512 devices in a mesh: shard: 32 (over y_hi, z), layer: 16 (over x, y_lo, core).
Axes of the slice: x: 4, y: 8 (y_hi: 4, y_lo: 2; y = y_hi * 2 + y_lo), z: 8, core: 2. Of those that a mesh axis runs over, the one named last changes fastest.
Arguments:
- query_grads: bfloat16 [128, 48, 4096], P('shard', 'layer'), may hold values from -12 to 12
- out_basis: float32 [48, 64, 64], P('layer'), may hold values from -0.2 to 1.2
- in_basis: float32 [48, 64, 64], P('layer'), may hold values from -0.2 to 1.2
- eigen_scale: float32 [48, 64, 64], P('layer'), may hold values from 0.05 to 5
- layer_slot: int32 [48], P('layer'), may hold values from 0 to 47, as said below
- train_grads: bfloat16 [1024, 48, 4096], P('shard', 'layer'), may hold values from -6 to 6
Outputs:
- scores: float32 [128, 1024], P('layer', 'shard')
The draws below stay inside these ranges and needn't reach their ends.
Inputs may be any that keep to these rules, and one draw needn't show every extreme that they name: `layer_slot`: slot s holds one of the layers s - s % 3 to s - s % 3 + 2, and each layer is held by exactly one slot.
All inputs are finite; a program needn't handle non-finite values.
Results may differ from the reference program's by a relative error of at most 0.0029.
Values may be sent and summed in bfloat16 or wider, within the bound.
A program may use at most 64 MiB of HBM per device.

```python
import math
import jax
import jax.numpy as jnp
from jax import lax

K = 64
F = 4096
LPD = 3
LAYERS = 48
QUERIES = 128
TRAIN = 1024


def draw_query_grads(key, part):
    key = jax.random.fold_in(key, 11)
    position = jnp.arange(LAYERS, dtype=jnp.float32)
    growth = 3.0 ** (position / max(LAYERS - 1, 1))
    base = jax.random.truncated_normal(key, -4.0, 4.0, (QUERIES, LAYERS, F))
    return (base * growth[None, :, None]).astype(jnp.bfloat16)


def basis_from(key):
    noise = 0.05 * jax.random.truncated_normal(key, -4.0, 4.0, (LAYERS, K, K))
    return (jnp.eye(K, dtype=jnp.float32)[None] + noise).astype(jnp.float32)


def draw_out_basis(key, part):
    key = jax.random.fold_in(key, 23)
    return basis_from(key)


def draw_in_basis(key, part):
    key = jax.random.fold_in(key, 37)
    return basis_from(key)


def draw_layer_slot(key, part):
    key = jax.random.fold_in(key, 5)
    groups = LAYERS // LPD
    keys = jax.random.split(key, groups)
    orders = jax.vmap(lambda single: jax.random.permutation(single, LPD))(keys)
    offsets = jnp.arange(groups, dtype=jnp.int32)[:, None] * LPD
    return (orders.astype(jnp.int32) + offsets).reshape(LAYERS).astype(jnp.int32)


def levels(stream_key, dims, cuts, smallest, largest):
    loudness = 1.0
    for axis_at, parts in cuts:
        draws = jax.random.uniform(jax.random.fold_in(jax.random.fold_in(stream_key, 6), axis_at), (parts,), jnp.float32, smallest / len(cuts), largest / len(cuts))
        loudness = loudness * jnp.repeat(jnp.exp(draws), dims[axis_at] // parts).reshape((-1,) + (1,) * (len(dims) - 1 - axis_at))
    return loudness


def scatter_about(own_key, extent, scale, most, cuts=(), kind=jnp.bfloat16):
    loudness = levels(own_key, extent, cuts, -0.22, 0.18) if cuts else 1.0
    values = jax.random.normal(own_key, extent, jnp.float32) * scale * loudness
    return jnp.minimum(jnp.maximum(values, -most), most).astype(kind)


def setup_inputs(seed: int = 0) -> dict:
    key_of = jax.random.split(jax.random.key(seed), 7)
    query_grads = draw_query_grads(jax.random.fold_in(key_of[6], 71), 0)
    out_basis = draw_out_basis(jax.random.fold_in(key_of[6], 71), 0)
    in_basis = draw_in_basis(jax.random.fold_in(key_of[6], 71), 0)
    eigen_scale = jnp.clip(jnp.exp(math.log(5.0) - 4.6051702 * jax.random.uniform(key_of[3], (LAYERS, K, K), jnp.float32) ** levels(key_of[3], (LAYERS, K, K), ((0, 16),), -0.2, 0.2)), 0.05, 5.0)
    layer_slot = draw_layer_slot(jax.random.fold_in(key_of[6], 71), 0)
    train_grads = scatter_about(key_of[5], (TRAIN, LAYERS, F), 1.0, 6.0, ((0, 32), (1, 16)))
    return {"query_grads": query_grads, "out_basis": out_basis, "in_basis": in_basis, "eigen_scale": eigen_scale, "layer_slot": layer_slot, "train_grads": train_grads}


DAMPING = 0.05
EPSILON = 1e-06

def precondition_layer(blocks, left_basis, right_basis, eigen_values):
    high = lax.Precision.HIGHEST
    rotated = jnp.einsum('ab,nac->nbc', left_basis, blocks, precision=high)
    rotated = jnp.einsum('nbc,cd->nbd', rotated, right_basis, precision=high)
    rotated = rotated / (eigen_values + DAMPING)
    back = jnp.einsum('ab,nbd->nad', left_basis, rotated, precision=high)
    return jnp.einsum('nad,cd->nac', back, right_basis, precision=high)

def reference(query_grads, out_basis, in_basis, eigen_scale, layer_slot, train_grads):
    count = query_grads.shape[0]
    width = query_grads.shape[2]
    pieces = []
    for layer_index in range(LAYERS):
        blocks = query_grads[:, layer_index].astype(jnp.float32).reshape(count, K, K)
        result = precondition_layer(blocks, out_basis[layer_index], in_basis[layer_index], eigen_scale[layer_index])
        pieces.append(result.reshape(count, width).astype(jnp.bfloat16))
    precond = jnp.stack(pieces, axis=1)
    wide = precond.astype(jnp.float32)
    norm = lax.optimization_barrier(jnp.sum(wide * wide, axis=(1, 2)))
    ordered = jnp.take(precond, layer_slot.astype(jnp.int32), axis=1)
    raw = lax.dot_general(ordered.reshape(count, LAYERS * width), train_grads.reshape(train_grads.shape[0], LAYERS * width), (((1,), (1,)), ((), ())), preferred_element_type=jnp.float32)
    return raw / jnp.sqrt(norm + EPSILON)[:, None]
```

```python
import functools

import jax
import jax.numpy as jnp
from jax import lax
from jax.experimental import pallas as pl
from jax.experimental.pallas import tpu as pltpu
from jax.sharding import PartitionSpec as P

DAMPING = 0.05
EPSILON = 1e-06
MESH = pl.DeviceIdType.MESH
COLUMNS = 4
OWN, FIRST, SECOND, ACROSS = range(4)


def precondition_slot(index, slot, q_ref, s_ref, a_ref, e_ref, rows_ref, turned_ref, blocks_ref):
    high = lax.Precision.HIGHEST
    side = s_ref.shape[1]
    width = q_ref.shape[2]
    pieces = width // 128
    quarter = pieces // 8
    queries = q_ref[index].astype(jnp.float32)
    for piece in range(pieces):
        rows_ref[slot, 4 * piece : 4 * piece + 4, :] = queries[:, 128 * piece : 128 * (piece + 1)]
    count = side // 4
    basis = jnp.concatenate(
        [s_ref[index, pl.ds(2 * parity + half, count, stride=4), :] for half in range(2) for parity in range(2)], axis=0
    )
    right = a_ref[index]
    scale = e_ref[index] + DAMPING
    stacked = []
    for n in range(4):
        halves = [rows_ref[slot, pl.ds(4 * parity + n, count, stride=8), :] for parity in range(2)]
        both = jnp.concatenate(halves, axis=0)
        stacked.append(jnp.concatenate([both[:, :side], both[:, side:]], axis=0))
    stacked = jnp.concatenate(stacked, axis=0)
    stacked = lax.dot_general(stacked, right, (((1,), (0,)), ((), ())), precision=high, preferred_element_type=jnp.float32)
    wide = jnp.concatenate([stacked[side * n : side * (n + 1)] for n in range(4)], axis=1)
    wide = lax.dot_general(basis.T, wide, (((1,), (0,)), ((), ())), precision=high, preferred_element_type=jnp.float32)
    wide = wide / jnp.concatenate([scale] * 4, axis=1)
    wide = lax.dot_general(basis, wide, (((1,), (0,)), ((), ())), precision=high, preferred_element_type=jnp.float32)
    stacked = jnp.concatenate([wide[:, side * n : side * (n + 1)] for n in range(4)], axis=0)
    stacked = lax.dot_general(stacked, right, (((1,), (1,)), ((), ())), precision=high, preferred_element_type=jnp.float32)
    for n in range(4):
        block = stacked[side * n : side * (n + 1)]
        lanes = jnp.concatenate([block[: side // 2], block[side // 2 :]], axis=1)
        for parity in range(2):
            turned_ref[slot, parity, pl.ds(n, count, stride=4), :] = lanes[count * parity : count * (parity + 1)]
    for parity in range(2):
        for part in range(4):
            blocks_ref[part, :, 256 * slot + 128 * parity : 256 * slot + 128 * (parity + 1)] = turned_ref[
                slot, parity, 16 * part : 16 * (part + 1), :
            ].astype(jnp.bfloat16)


def kernel(
    ring,
    groups,
    slot_ref,
    q_ref,
    s_ref,
    a_ref,
    e_ref,
    train_ref,
    out_ref,
    rows_ref,
    turned_ref,
    blocks_ref,
    train_part,
    gathered,
    total,
    squares,
    tiles,
    tiles_in,
    summed,
    summed_in,
    local_sem,
    t_send,
    t_recv,
    y_send,
    y_recv,
    z_send,
    z_recv,
    r_send,
    r_recv,
    p_send,
    p_recv,
):
    shard = lax.axis_index("shard")
    group = lax.axis_index("layer")
    column = shard // ring
    level = lax.rem(shard, ring)
    slots = q_ref.shape[0]
    reach = ring // 2
    tile_count = tiles.shape[0]

    def at(col, lev):
        return col * ring + lev

    first = column + 1 - 2 * lax.rem(column, 2)
    second = 3 - column
    across = 3 - first
    columns = [column, first, second, across]
    high_first = jnp.where((column == 1) | (column == 2), 1, 0)
    high_second = jnp.where(column >= 2, 1, 0)
    mine = [high_first, 2 + high_second]
    other = [1 - high_first, 3 - high_second]

    def remote(src, dst, send, recv, to_shard, to_group):
        return pltpu.make_async_remote_copy(
            src_ref=src, dst_ref=dst, send_sem=send, recv_sem=recv, device_id=(to_shard, to_group), device_id_type=MESH
        )

    up = at(column, lax.rem(level + 1, ring))
    down = at(column, lax.rem(level + ring - 1, ring))
    barrier = pltpu.get_barrier_semaphore()
    partners = [(up, group), (down, group)] + [(at(c, level), group) for c in columns[1:]]
    partners += [(shard, lax.rem(group + d, groups)) for d in range(1, groups)]
    for who in partners:
        pl.semaphore_signal(barrier, inc=1, device_id=who, device_id_type=MESH)
    pl.semaphore_wait(barrier, len(partners))

    span = train_ref.shape[2] // 4

    def quarter_of_train(quarter):
        return train_ref.at[:, :, pl.ds(pl.multiple_of(quarter * span, 128), span)]

    train_copies = []
    for pair in range(2):
        copy = remote(
            quarter_of_train(other[pair]),
            train_part.at[pair, 1],
            t_send.at[pair],
            t_recv.at[pair],
            at(columns[1 + pair], level),
            group,
        )
        copy.start()
        train_copies.append(copy)
    keep = []
    for pair in range(2):
        copy = pltpu.make_async_copy(quarter_of_train(mine[pair]), train_part.at[pair, 0], local_sem.at[pair])
        copy.start()
        keep.append(copy)

    for slot in range(slots):
        index = lax.rem(slot_ref[slot], slots)
        precondition_slot(index, slot, q_ref, s_ref, a_ref, e_ref, rows_ref, turned_ref, blocks_ref)

    wanted = {FIRST: [other[0], mine[1]], SECOND: [mine[0], other[1]], ACROSS: other}
    column_copies = {}
    for who in (FIRST, SECOND, ACROSS):
        for pair in range(2):
            copy = remote(
                blocks_ref.at[wanted[who][pair]],
                gathered.at[pair, column, level],
                y_send.at[who - 1, pair],
                y_recv.at[who - 1, pair],
                at(columns[who], level),
                group,
            )
            copy.start()
            column_copies[who, pair] = copy
    for pair in range(2):
        gathered[pair, column, level] = blocks_ref[mine[pair]]

    ring_copies = {}

    def runs(way, hop, who):
        return hop < reach or (who // 2 == way)

    def origin(way, hop):
        return lax.rem(level - hop + ring, ring) if way == 0 else lax.rem(level + hop, ring)

    def pass_on(way, hop, who):
        block = gathered.at[:, columns[who], origin(way, hop - 1)]
        copy = remote(
            block, block, z_send.at[way, hop - 1, who], z_recv.at[way, hop - 1, who], up if way == 0 else down, group
        )
        copy.start()
        ring_copies[way, hop, who] = copy

    def arrive(way, hop, who):
        block = gathered.at[:, columns[who], origin(way, hop)]
        remote(
            block, block, z_send.at[way, hop - 1, who], z_recv.at[way, hop - 1, who], up if way == 0 else down, group
        ).wait_recv()

    for who in (OWN, FIRST, SECOND, ACROSS):
        if who != OWN:
            for pair in range(2):
                remote(
                    blocks_ref.at[0],
                    gathered.at[pair, columns[who], level],
                    y_send.at[who - 1, pair],
                    y_recv.at[who - 1, pair],
                    at(columns[who], level),
                    group,
                ).wait_recv()
        for way in range(2):
            if runs(way, 1, who):
                pass_on(way, 1, who)

    def multiply(levels):
        for pair in range(2):
            left = [gathered[pair, :, pl.ds(lev, 1)].reshape(16 * COLUMNS, 256 * slots) for lev in levels]
            left = jnp.concatenate(left, axis=0) if len(left) > 1 else left[0]
            product = None
            for slot in range(slots):
                right = jnp.concatenate(
                    [
                        train_part[pair, who, slot, :, 256 * sub : 256 * (sub + 1)]
                        for who in range(2)
                        for sub in range(4)
                    ],
                    axis=0,
                )
                term = lax.dot_general(
                    left[:, 256 * slot : 256 * (slot + 1)],
                    right,
                    (((1,), (1,)), ((), ())),
                    preferred_element_type=jnp.float32,
                )
                product = term if product is None else product + term
            wide = left.astype(jnp.float32)
            wide = wide * wide
            norm = wide[:, :128]
            for piece in range(1, 2 * slots):
                norm = norm + wide[:, 128 * piece : 128 * (piece + 1)]
            row = lax.broadcasted_iota(jnp.int32, (16, product.shape[1]), 0) // 4
            lane = lax.rem(lax.broadcasted_iota(jnp.int32, (16, product.shape[1]), 1), 128) // 32
            same = row == lane
            for at_level, lev in enumerate(levels):
                for col in range(COLUMNS):
                    start = 16 * (COLUMNS * at_level + col)
                    kept = jnp.where(same, product[start : start + 16], 0.0)
                    total[pair, col, lev] = kept[:8] + kept[8:]
                    squares[pair, col, lev] = norm[start : start + 8] + norm[start + 8 : start + 16]

    for hop in range(1, reach + 1):
        for who in range(4):
            for way in range(2):
                if runs(way, hop, who):
                    arrive(way, hop, who)
                    if hop < reach and runs(way, hop + 1, who):
                        pass_on(way, hop + 1, who)
        if hop == 1:
            for copy in keep:
                copy.wait()
            for copy in train_copies:
                copy.wait_recv()
            multiply([level])
        if hop < reach:
            multiply([origin(0, hop), origin(1, hop)])
        else:
            multiply([origin(0, hop)])

    row = lax.broadcasted_iota(jnp.int32, (8, 128), 0)
    lane = lax.broadcasted_iota(jnp.int32, (8, 128), 1)

    def fold(value):
        value = value + pltpu.roll(value, 64, 1)
        return value + pltpu.roll(value, 32, 1)

    per_column = ring // 2
    for tile in range(tile_count):
        col, pair_of_levels = tile // per_column, tile % per_column

        def rows_of(ref, pair, lanes):
            even, odd = (ref[pair, col, 2 * pair_of_levels + k, :, lanes] for k in range(2))
            even = even + pltpu.roll(even, 4, 0)
            odd = odd + pltpu.roll(odd, 4, 0)
            return jnp.where(row < 4, even, odd)

        own = fold(rows_of(total, 0, slice(0, 128)) + rows_of(total, 1, slice(0, 128)))
        one = fold(rows_of(total, 0, slice(128, 256)))
        two = fold(rows_of(total, 1, slice(128, 256)))
        norm_one = jnp.sum(rows_of(squares, 0, slice(0, 128)), axis=1, keepdims=True)
        norm_two = jnp.sum(rows_of(squares, 1, slice(0, 128)), axis=1, keepdims=True)
        value = jnp.where(lane < 32, own, jnp.where(lane < 64, one, jnp.where(lane < 96, two, jnp.where(lane < 112, norm_one, norm_two))))
        tiles[tile] = value

    per_group = tile_count // groups
    group_copies = []
    for d in range(1, groups):
        to = lax.rem(group + d, groups)
        copy = remote(tiles.at[pl.ds(to * per_group, per_group)], tiles_in.at[d], r_send.at[d], r_recv.at[d], shard, to)
        copy.start()
        group_copies.append(copy)
    answer = tiles[pl.ds(group * per_group, per_group)]
    for copy in group_copies:
        copy.wait_recv()
    for d in range(1, groups):
        answer = answer + tiles_in[d]
    summed[...] = answer
    pair_copies = []
    for pair in range(2):
        copy = remote(summed, summed_in.at[pair], p_send.at[pair], p_recv.at[pair], at(columns[1 + pair], level), group)
        copy.start()
        pair_copies.append(copy)
    for copy in pair_copies:
        copy.wait_recv()
    from_first = summed_in[0]
    from_second = summed_in[1]
    norm = answer[:, :, 96:97] + answer[:, :, 112:113] + from_first[:, :, 96:97] + from_second[:, :, 112:113]
    raw = answer[:, :, 0:32] + from_first[:, :, 32:64] + from_second[:, :, 64:96]
    out_ref[...] = (raw / jnp.sqrt(norm + EPSILON)).reshape(out_ref.shape)

    for copy in train_copies + list(column_copies.values()) + list(ring_copies.values()) + group_copies + pair_copies:
        copy.wait_send()


def solution(mesh):
    shards, groups = mesh.shape["shard"], mesh.shape["layer"]
    ring = shards // COLUMNS

    def on_device(query_grads, out_basis, in_basis, eigen_scale, layer_slot, train_grads):
        local, slots, width = query_grads.shape
        rows = train_grads.shape[0]
        tile_count = local * shards // 8
        per_group = tile_count // groups
        reach = ring // 2
        vmem = pl.BlockSpec(memory_space=pltpu.VMEM)
        dma = pltpu.SemaphoreType.DMA
        return pl.pallas_call(
            functools.partial(kernel, ring, groups),
            out_shape=jax.ShapeDtypeStruct((8 * per_group, rows), jnp.float32),
            in_specs=[pl.BlockSpec(memory_space=pltpu.SMEM), vmem, vmem, vmem, vmem, pl.BlockSpec(memory_space=pl.ANY)],
            out_specs=vmem,
            scratch_shapes=[
                pltpu.VMEM((slots, local * width // 128, 128), jnp.float32),
                pltpu.VMEM((slots, 2, local * width // 256, 128), jnp.float32),
                pltpu.VMEM((4, 16, 256 * slots), jnp.bfloat16),
                pltpu.VMEM((2, 2, slots, rows, width // 4), jnp.bfloat16),
                pltpu.VMEM((2, COLUMNS, ring, 16, 256 * slots), jnp.bfloat16),
                pltpu.VMEM((2, COLUMNS, ring, 8, 256), jnp.float32),
                pltpu.VMEM((2, COLUMNS, ring, 8, 128), jnp.float32),
                pltpu.VMEM((tile_count, 8, 128), jnp.float32),
                pltpu.VMEM((groups, per_group, 8, 128), jnp.float32),
                pltpu.VMEM((per_group, 8, 128), jnp.float32),
                pltpu.VMEM((2, per_group, 8, 128), jnp.float32),
                dma((2,)),
                dma((2,)),
                dma((2,)),
                dma((3, 2)),
                dma((3, 2)),
                dma((2, reach, 4)),
                dma((2, reach, 4)),
                dma((groups,)),
                dma((groups,)),
                dma((2,)),
                dma((2,)),
            ],
            compiler_params=pltpu.CompilerParams(
                collective_id=0, has_side_effects=True, vmem_limit_bytes=32 * 1024 * 1024
            ),
        )(
            layer_slot,
            jnp.transpose(query_grads, (1, 0, 2)),
            out_basis,
            in_basis,
            eigen_scale,
            jnp.transpose(train_grads, (1, 0, 2)),
        )

    return jax.shard_map(
        on_device,
        mesh=mesh,
        in_specs=(
            P("shard", "layer", None),
            P("layer", None, None),
            P("layer", None, None),
            P("layer", None, None),
            P("layer"),
            P("shard", "layer", None),
        ),
        out_specs=P("layer", "shard"),
        check_vma=False,
    )
```

```python
import functools

import jax
import jax.numpy as jnp
from jax import lax
from jax.experimental import pallas as pl
from jax.experimental.pallas import tpu as pltpu
from jax.sharding import PartitionSpec as P

DAMPING = 0.05
EPSILON = 1e-06
MESH = pl.DeviceIdType.MESH
COLUMNS = 4
OWN, FIRST, SECOND, ACROSS = range(4)
NEAR = (2, -2, 1, -1)
VMEM_BYTES = 63 * 1024 * 1024


def precondition_slot(index, slot, q_ref, s_ref, a_ref, e_ref, rows_ref, turned_ref, blocks_ref):
    high = lax.Precision.HIGHEST
    side = s_ref.shape[1]
    width = q_ref.shape[2]
    pieces = width // 128
    quarter = pieces // 8
    queries = q_ref[index].astype(jnp.float32)
    for piece in range(pieces):
        rows_ref[slot, 4 * piece : 4 * piece + 4, :] = queries[:, 128 * piece : 128 * (piece + 1)]
    count = side // 4
    basis = jnp.concatenate(
        [s_ref[index, pl.ds(2 * parity + half, count, stride=4), :] for half in range(2) for parity in range(2)], axis=0
    )
    right = a_ref[index]
    scale = e_ref[index] + DAMPING
    stacked = []
    for n in range(4):
        halves = [rows_ref[slot, pl.ds(4 * parity + n, count, stride=8), :] for parity in range(2)]
        both = jnp.concatenate(halves, axis=0)
        stacked.append(jnp.concatenate([both[:, :side], both[:, side:]], axis=0))
    stacked = jnp.concatenate(stacked, axis=0)
    stacked = lax.dot_general(stacked, right, (((1,), (0,)), ((), ())), precision=high, preferred_element_type=jnp.float32)
    wide = jnp.concatenate([stacked[side * n : side * (n + 1)] for n in range(4)], axis=1)
    wide = lax.dot_general(basis.T, wide, (((1,), (0,)), ((), ())), precision=high, preferred_element_type=jnp.float32)
    wide = wide / jnp.concatenate([scale] * 4, axis=1)
    wide = lax.dot_general(basis, wide, (((1,), (0,)), ((), ())), precision=high, preferred_element_type=jnp.float32)
    stacked = jnp.concatenate([wide[:, side * n : side * (n + 1)] for n in range(4)], axis=0)
    stacked = lax.dot_general(stacked, right, (((1,), (1,)), ((), ())), precision=high, preferred_element_type=jnp.float32)
    for n in range(4):
        block = stacked[side * n : side * (n + 1)]
        lanes = jnp.concatenate([block[: side // 2], block[side // 2 :]], axis=1)
        for parity in range(2):
            turned_ref[slot, parity, pl.ds(n, count, stride=4), :] = lanes[count * parity : count * (parity + 1)]
    for parity in range(2):
        for part in range(4):
            blocks_ref[part, :, 256 * slot + 128 * parity : 256 * slot + 128 * (parity + 1)] = turned_ref[
                slot, parity, 16 * part : 16 * (part + 1), :
            ].astype(jnp.bfloat16)


def kernel(
    ring,
    groups,
    slot_hbm,
    q_hbm,
    s_hbm,
    a_hbm,
    e_hbm,
    train_ref,
    out_ref,
    slot_ref,
    q_ref,
    s_ref,
    a_ref,
    e_ref,
    rows_ref,
    turned_ref,
    blocks_ref,
    train_part,
    gathered,
    total,
    squares,
    tiles,
    tiles_in,
    summed,
    summed_in,
    local_sem,
    t_send,
    t_recv,
    y_send,
    y_recv,
    near_send,
    near_recv,
    far_send,
    far_recv,
    r_send,
    r_recv,
    p_send,
    p_recv,
):
    shard = lax.axis_index("shard")
    group = lax.axis_index("layer")
    column = shard // ring
    level = lax.rem(shard, ring)
    slots = q_ref.shape[0]
    tile_count = tiles.shape[0]

    def at(col, lev):
        return col * ring + lev

    def shifted(by):
        return lax.rem(level + by + ring, ring)

    first = column + 1 - 2 * lax.rem(column, 2)
    second = 3 - column
    across = 3 - first
    columns = [column, first, second, across]

    def remote(src, dst, send, recv, to_shard, to_group):
        return pltpu.make_async_remote_copy(
            src_ref=src, dst_ref=dst, send_sem=send, recv_sem=recv, device_id=(to_shard, to_group), device_id_type=MESH
        )

    loads = []
    for i, (src, dst) in enumerate(
        [(q_hbm, q_ref), (a_hbm, a_ref), (s_hbm, s_ref), (e_hbm, e_ref), (slot_hbm, slot_ref)]
    ):
        copy = pltpu.make_async_copy(src, dst, local_sem.at[i])
        copy.start()
        loads.append(copy)

    span = train_ref.shape[2] // COLUMNS

    def quarter_of_train(quarter):
        return train_ref.at[:, :, pl.ds(pl.multiple_of(quarter * span, 128), span)]

    keep = pltpu.make_async_copy(quarter_of_train(column), train_part.at[OWN], local_sem.at[len(loads)])
    keep.start()

    barrier = pltpu.get_barrier_semaphore()
    partners = [(at(column, shifted(by)), group) for by in NEAR]
    partners += [(at(c, level), group) for c in columns[1:]]
    partners += [(shard, lax.rem(group + d, groups)) for d in range(1, groups)]
    for who in partners:
        pl.semaphore_signal(barrier, inc=1, device_id=who, device_id_type=MESH)
    pl.semaphore_wait(barrier, len(partners))

    train_copies = []
    for who in (FIRST, SECOND, ACROSS):
        copy = remote(
            quarter_of_train(columns[who]), train_part.at[who], t_send.at[who], t_recv.at[who], at(columns[who], level), group
        )
        copy.start()
        train_copies.append(copy)

    for copy in loads:
        copy.wait()
    for slot in range(slots):
        index = lax.rem(slot_ref[slot], slots)
        precondition_slot(index, slot, q_ref, s_ref, a_ref, e_ref, rows_ref, turned_ref, blocks_ref)

    column_copies = []
    for who in (FIRST, SECOND, ACROSS):
        copy = remote(
            blocks_ref.at[columns[who]],
            gathered.at[column, level],
            y_send.at[who],
            y_recv.at[who],
            at(columns[who], level),
            group,
        )
        copy.start()
        column_copies.append(copy)
    gathered[column, level] = blocks_ref[column]

    def block_of(who, by):
        return gathered.at[columns[who], shifted(by)]

    near_copies, far_copies = [], []
    for who in range(COLUMNS):
        if who != OWN:
            remote(
                blocks_ref.at[0], block_of(who, 0), y_send.at[who], y_recv.at[who], at(columns[who], level), group
            ).wait_recv()
        for i, by in enumerate(NEAR):
            copy = remote(
                block_of(who, 0), block_of(who, 0), near_send.at[i, who], near_recv.at[i, who], at(column, shifted(by)), group
            )
            copy.start()
            near_copies.append(copy)

    def near_arrive(i, who):
        block = block_of(who, -NEAR[i])
        remote(block, block, near_send.at[i, who], near_recv.at[i, who], at(column, shifted(NEAR[i])), group).wait_recv()

    far = [(0, -2, 1, range(4)), (1, 2, -1, range(4)), (2, -2, 2, (0, 1)), (3, 2, -2, (2, 3))]
    for who in range(COLUMNS):
        for i, by in enumerate(NEAR[:2]):
            near_arrive(i, who)
            for row, source, on, which in far:
                if source == -by and who in which:
                    block = block_of(who, source)
                    copy = remote(
                        block, block, far_send.at[row, who], far_recv.at[row, who], at(column, shifted(on)), group
                    )
                    copy.start()
                    far_copies.append(copy)
    for who in range(COLUMNS):
        for i in range(2, len(NEAR)):
            near_arrive(i, who)

    def multiply(levels):
        left = [gathered[:, pl.ds(lev, 1)].reshape(16 * COLUMNS, 256 * slots) for lev in levels]
        left = jnp.concatenate(left, axis=0) if len(left) > 1 else left[0]
        wide = left.astype(jnp.float32)
        wide = wide * wide
        norm = wide[:, :128]
        for piece in range(1, 2 * slots):
            norm = norm + wide[:, 128 * piece : 128 * (piece + 1)]
        row = lax.broadcasted_iota(jnp.int32, (16, 128), 0) // 4
        lane = lax.broadcasted_iota(jnp.int32, (16, 128), 1) // 32
        same = row == lane
        for who in range(COLUMNS):
            product = None
            for slot in range(slots):
                right = jnp.concatenate(
                    [train_part[who, slot, :, 256 * sub : 256 * (sub + 1)] for sub in range(4)], axis=0
                )
                term = lax.dot_general(
                    left[:, 256 * slot : 256 * (slot + 1)],
                    right,
                    (((1,), (1,)), ((), ())),
                    preferred_element_type=jnp.float32,
                )
                product = term if product is None else product + term
            for at_level, lev in enumerate(levels):
                for col in range(COLUMNS):
                    start = 16 * (COLUMNS * at_level + col)
                    kept = jnp.where(same, product[start : start + 16], 0.0)
                    total[col, lev, :, 128 * who : 128 * (who + 1)] = kept[:8] + kept[8:]
        for at_level, lev in enumerate(levels):
            for col in range(COLUMNS):
                start = 16 * (COLUMNS * at_level + col)
                squares[col, lev] = norm[start : start + 8] + norm[start + 8 : start + 16]

    keep.wait()
    for copy in train_copies:
        copy.wait_recv()
    multiply([level] + [shifted(by) for by in NEAR])
    for row, source, on, which in far:
        for who in which:
            block = block_of(who, source - on)
            remote(block, block, far_send.at[row, who], far_recv.at[row, who], at(column, shifted(on)), group).wait_recv()
    multiply([shifted(by) for by in (3, 4, 5)])

    row = lax.broadcasted_iota(jnp.int32, (8, 128), 0)
    lane = lax.broadcasted_iota(jnp.int32, (8, 128), 1) // 32

    def fold(value):
        value = value + pltpu.roll(value, 64, 1)
        return value + pltpu.roll(value, 32, 1)

    per_column = ring // 2

    def make_tile(tile, carry):
        col, pair_of_levels = tile // per_column, lax.rem(tile, per_column)

        def rows_of(ref, lanes):
            even, odd = (ref[col, 2 * pair_of_levels + k, :, lanes] for k in range(2))
            even = even + pltpu.roll(even, 4, 0)
            odd = odd + pltpu.roll(odd, 4, 0)
            return jnp.where(row < 4, even, odd)

        value = fold(rows_of(total, slice(0, 128)))
        for who in range(1, COLUMNS):
            value = jnp.where(lane < who, value, fold(rows_of(total, slice(128 * who, 128 * (who + 1)))))
        norm = jnp.sum(rows_of(squares, slice(0, 128)), axis=1, keepdims=True)
        tiles[tile, :, :128] = value
        tiles[tile, :, 128:] = jnp.broadcast_to(norm, value.shape)
        return carry

    lax.fori_loop(0, tile_count, make_tile, 0)

    per_group = tile_count // groups
    group_copies = []
    for d in range(1, groups):
        to = lax.rem(group + d, groups)
        copy = remote(tiles.at[pl.ds(to * per_group, per_group)], tiles_in.at[d], r_send.at[d], r_recv.at[d], shard, to)
        copy.start()
        group_copies.append(copy)
    answer = tiles[pl.ds(group * per_group, per_group)]
    for copy in group_copies:
        copy.wait_recv()
    for d in range(1, groups):
        answer = answer + tiles_in[d]
    summed[...] = answer
    pair_copies = []
    for who in (FIRST, SECOND, ACROSS):
        copy = remote(summed, summed_in.at[who], p_send.at[who], p_recv.at[who], at(columns[who], level), group)
        copy.start()
        pair_copies.append(copy)
    for copy in pair_copies:
        copy.wait_recv()
    raw, norm = answer[:, :, :32], answer[:, :, 128:129]
    for who in (FIRST, SECOND, ACROSS):
        raw = raw + summed_in[who, :, :, 32 * who : 32 * (who + 1)]
        norm = norm + summed_in[who, :, :, 128:129]
    out_ref[...] = (raw / jnp.sqrt(norm + EPSILON)).reshape(out_ref.shape)

    for copy in train_copies + column_copies + near_copies + far_copies + group_copies + pair_copies:
        copy.wait_send()


def solution(mesh):
    shards, groups = mesh.shape["shard"], mesh.shape["layer"]
    ring = shards // COLUMNS

    def on_device(query_grads, out_basis, in_basis, eigen_scale, layer_slot, train_grads):
        local, slots, width = query_grads.shape
        side = out_basis.shape[1]
        rows = train_grads.shape[0]
        tile_count = local * shards // 8
        per_group = tile_count // groups
        dma = pltpu.SemaphoreType.DMA
        return pl.pallas_call(
            functools.partial(kernel, ring, groups),
            out_shape=jax.ShapeDtypeStruct((8 * per_group, rows), jnp.float32),
            in_specs=[pl.BlockSpec(memory_space=pl.ANY)] * 6,
            out_specs=pl.BlockSpec(memory_space=pltpu.VMEM),
            scratch_shapes=[
                pltpu.SMEM((slots,), jnp.int32),
                pltpu.VMEM((slots, local, width), jnp.bfloat16),
                pltpu.VMEM((slots, side, side), jnp.float32),
                pltpu.VMEM((slots, side, side), jnp.float32),
                pltpu.VMEM((slots, side, side), jnp.float32),
                pltpu.VMEM((slots, local * width // 128, 128), jnp.float32),
                pltpu.VMEM((slots, 2, local * width // 256, 128), jnp.float32),
                pltpu.VMEM((COLUMNS, 16, 256 * slots), jnp.bfloat16),
                pltpu.VMEM((COLUMNS, slots, rows, width // COLUMNS), jnp.bfloat16),
                pltpu.VMEM((COLUMNS, ring, 16, 256 * slots), jnp.bfloat16),
                pltpu.VMEM((COLUMNS, ring, 8, 128 * COLUMNS), jnp.float32),
                pltpu.VMEM((COLUMNS, ring, 8, 128), jnp.float32),
                pltpu.VMEM((tile_count, 8, 256), jnp.float32),
                pltpu.VMEM((groups, per_group, 8, 256), jnp.float32),
                pltpu.VMEM((per_group, 8, 256), jnp.float32),
                pltpu.VMEM((COLUMNS, per_group, 8, 256), jnp.float32),
                dma((6,)),
                dma((COLUMNS,)),
                dma((COLUMNS,)),
                dma((COLUMNS,)),
                dma((COLUMNS,)),
                dma((4, COLUMNS)),
                dma((4, COLUMNS)),
                dma((4, COLUMNS)),
                dma((4, COLUMNS)),
                dma((groups,)),
                dma((groups,)),
                dma((COLUMNS,)),
                dma((COLUMNS,)),
            ],
            compiler_params=pltpu.CompilerParams(
                collective_id=0, has_side_effects=True, vmem_limit_bytes=VMEM_BYTES
            ),
        )(
            layer_slot,
            jnp.transpose(query_grads, (1, 0, 2)),
            out_basis,
            in_basis,
            eigen_scale,
            jnp.transpose(train_grads, (1, 0, 2)),
        )

    return jax.shard_map(
        on_device,
        mesh=mesh,
        in_specs=(
            P("shard", "layer", None),
            P("layer", None, None),
            P("layer", None, None),
            P("layer", None, None),
            P("layer"),
            P("shard", "layer", None),
        ),
        out_specs=P("layer", "shard"),
        check_vma=False,
    )
```

```python
import functools

import jax
import jax.numpy as jnp
from jax import lax
from jax.experimental import pallas as pl
from jax.experimental.pallas import tpu as pltpu
from jax.sharding import PartitionSpec as P

DAMPING = 0.05
EPSILON = 1e-06
MESH = pl.DeviceIdType.MESH
COLUMNS = 4
OWN, FIRST, SECOND, ACROSS = range(4)
NEAR = (2, -2, 1, -1)
VMEM_BYTES = 63 * 1024 * 1024


def precondition_slot(index, slot, q_ref, s_ref, a_ref, e_ref, rows_ref, turned_ref, blocks_ref):
    high = lax.Precision.HIGHEST
    side = s_ref.shape[1]
    width = q_ref.shape[2]
    pieces = width // 128
    quarter = pieces // 8
    queries = q_ref[index].astype(jnp.float32)
    for piece in range(pieces):
        rows_ref[slot, 4 * piece : 4 * piece + 4, :] = queries[:, 128 * piece : 128 * (piece + 1)]
    count = side // 4
    basis = jnp.concatenate(
        [s_ref[index, pl.ds(2 * parity + half, count, stride=4), :] for half in range(2) for parity in range(2)], axis=0
    )
    right = a_ref[index]
    scale = e_ref[index] + DAMPING
    stacked = []
    for n in range(4):
        halves = [rows_ref[slot, pl.ds(4 * parity + n, count, stride=8), :] for parity in range(2)]
        both = jnp.concatenate(halves, axis=0)
        stacked.append(jnp.concatenate([both[:, :side], both[:, side:]], axis=0))
    stacked = jnp.concatenate(stacked, axis=0)
    stacked = lax.dot_general(stacked, right, (((1,), (0,)), ((), ())), precision=high, preferred_element_type=jnp.float32)
    wide = jnp.concatenate([stacked[side * n : side * (n + 1)] for n in range(4)], axis=1)
    wide = lax.dot_general(basis.T, wide, (((1,), (0,)), ((), ())), precision=high, preferred_element_type=jnp.float32)
    wide = wide / jnp.concatenate([scale] * 4, axis=1)
    wide = lax.dot_general(basis, wide, (((1,), (0,)), ((), ())), precision=high, preferred_element_type=jnp.float32)
    stacked = jnp.concatenate([wide[:, side * n : side * (n + 1)] for n in range(4)], axis=0)
    stacked = lax.dot_general(stacked, right, (((1,), (1,)), ((), ())), precision=high, preferred_element_type=jnp.float32)
    for n in range(4):
        block = stacked[side * n : side * (n + 1)]
        lanes = jnp.concatenate([block[: side // 2], block[side // 2 :]], axis=1)
        for parity in range(2):
            turned_ref[slot, parity, pl.ds(n, count, stride=4), :] = lanes[count * parity : count * (parity + 1)]
    for parity in range(2):
        for part in range(4):
            blocks_ref[part, :, 256 * slot + 128 * parity : 256 * slot + 128 * (parity + 1)] = turned_ref[
                slot, parity, 16 * part : 16 * (part + 1), :
            ].astype(jnp.bfloat16)


def kernel(
    ring,
    groups,
    slot_hbm,
    q_hbm,
    s_hbm,
    a_hbm,
    e_hbm,
    train_ref,
    out_ref,
    slot_ref,
    q_ref,
    s_ref,
    a_ref,
    e_ref,
    rows_ref,
    turned_ref,
    blocks_ref,
    train_part,
    gathered,
    total,
    squares,
    tiles,
    tiles_in,
    summed,
    summed_in,
    local_sem,
    t_send,
    t_recv,
    y_send,
    y_recv,
    near_send,
    near_recv,
    far_send,
    far_recv,
    r_send,
    r_recv,
    p_send,
    p_recv,
):
    shard = lax.axis_index("shard")
    group = lax.axis_index("layer")
    column = shard // ring
    level = lax.rem(shard, ring)
    slots = q_ref.shape[0]
    tile_count = tiles.shape[0]

    def at(col, lev):
        return col * ring + lev

    def shifted(by):
        return lax.rem(level + by + ring, ring)

    first = column + 1 - 2 * lax.rem(column, 2)
    second = 3 - column
    across = 3 - first
    columns = [column, first, second, across]

    def remote(src, dst, send, recv, to_shard, to_group):
        return pltpu.make_async_remote_copy(
            src_ref=src, dst_ref=dst, send_sem=send, recv_sem=recv, device_id=(to_shard, to_group), device_id_type=MESH
        )

    loads = []
    for i, (src, dst) in enumerate(
        [(q_hbm, q_ref), (a_hbm, a_ref), (s_hbm, s_ref), (e_hbm, e_ref), (slot_hbm, slot_ref)]
    ):
        copy = pltpu.make_async_copy(src, dst, local_sem.at[i])
        copy.start()
        loads.append(copy)

    span = train_ref.shape[2] // COLUMNS

    def quarter_of_train(quarter):
        return train_ref.at[:, :, pl.ds(pl.multiple_of(quarter * span, 128), span)]

    keep = pltpu.make_async_copy(quarter_of_train(column), train_part.at[OWN], local_sem.at[len(loads)])
    keep.start()

    barrier = pltpu.get_barrier_semaphore()
    partners = [(at(column, shifted(by)), group) for by in NEAR]
    partners += [(at(c, level), group) for c in columns[1:]]
    for who in partners:
        pl.semaphore_signal(barrier, inc=1, device_id=who, device_id_type=MESH)

    def greet(d, carry):
        pl.semaphore_signal(barrier, inc=1, device_id=(shard, lax.rem(group + d, groups)), device_id_type=MESH)
        return carry

    lax.fori_loop(1, groups, greet, 0)
    pl.semaphore_wait(barrier, len(partners) + groups - 1)

    train_copies = []

    def send_train(who, piece):
        lots = pl.ds(0, 1) if piece == 0 else pl.ds(1, slots - 1)
        copy = remote(
            quarter_of_train(columns[who]).at[lots],
            train_part.at[who, lots],
            t_send.at[who, piece],
            t_recv.at[who, piece],
            at(columns[who], level),
            group,
        )
        copy.start()
        train_copies.append(copy)

    for who in (FIRST, SECOND):
        send_train(who, 0)

    for copy in loads:
        copy.wait()
    for slot in range(slots):
        index = lax.rem(slot_ref[slot], slots)
        precondition_slot(index, slot, q_ref, s_ref, a_ref, e_ref, rows_ref, turned_ref, blocks_ref)

    column_copies = []
    for who in (FIRST, SECOND, ACROSS):
        copy = remote(
            blocks_ref.at[columns[who]],
            gathered.at[column, level],
            y_send.at[who],
            y_recv.at[who],
            at(columns[who], level),
            group,
        )
        copy.start()
        column_copies.append(copy)
    gathered[column, level] = blocks_ref[column]
    for who, piece in ((FIRST, 1), (SECOND, 1), (ACROSS, 0), (ACROSS, 1)):
        send_train(who, piece)

    def block_of(who, by):
        return gathered.at[columns[who], shifted(by)]

    near_copies, far_copies = [], []
    for who in range(COLUMNS):
        if who != OWN:
            remote(
                blocks_ref.at[0], block_of(who, 0), y_send.at[who], y_recv.at[who], at(columns[who], level), group
            ).wait_recv()
        for i, by in enumerate(NEAR):
            copy = remote(
                block_of(who, 0), block_of(who, 0), near_send.at[i, who], near_recv.at[i, who], at(column, shifted(by)), group
            )
            copy.start()
            near_copies.append(copy)

    def near_arrive(i, who):
        block = block_of(who, -NEAR[i])
        remote(block, block, near_send.at[i, who], near_recv.at[i, who], at(column, shifted(NEAR[i])), group).wait_recv()

    far = [(0, -2, 1, range(4)), (1, 2, -1, range(4)), (2, -2, 2, (0, 1)), (3, 2, -2, (2, 3))]
    for who in range(COLUMNS):
        for i, by in enumerate(NEAR[:2]):
            near_arrive(i, who)
            for row, source, on, which in far:
                if source == -by and who in which:
                    block = block_of(who, source)
                    copy = remote(
                        block, block, far_send.at[row, who], far_recv.at[row, who], at(column, shifted(on)), group
                    )
                    copy.start()
                    far_copies.append(copy)
    for who in range(COLUMNS):
        for i in range(2, len(NEAR)):
            near_arrive(i, who)

    def multiply(levels):
        left = [gathered[:, pl.ds(lev, 1)].reshape(16 * COLUMNS, 256 * slots) for lev in levels]
        left = jnp.concatenate(left, axis=0) if len(left) > 1 else left[0]
        wide = left.astype(jnp.float32)
        wide = wide * wide
        norm = wide[:, :128]
        for piece in range(1, 2 * slots):
            norm = norm + wide[:, 128 * piece : 128 * (piece + 1)]
        row = lax.broadcasted_iota(jnp.int32, (16, 128), 0) // 4
        lane = lax.broadcasted_iota(jnp.int32, (16, 128), 1) // 32
        same = row == lane
        for who in range(COLUMNS):
            product = None
            for slot in range(slots):
                right = jnp.concatenate(
                    [train_part[who, slot, :, 256 * sub : 256 * (sub + 1)] for sub in range(4)], axis=0
                )
                term = lax.dot_general(
                    left[:, 256 * slot : 256 * (slot + 1)],
                    right,
                    (((1,), (1,)), ((), ())),
                    preferred_element_type=jnp.float32,
                )
                product = term if product is None else product + term
            for at_level, lev in enumerate(levels):
                for col in range(COLUMNS):
                    start = 16 * (COLUMNS * at_level + col)
                    kept = jnp.where(same, product[start : start + 16], 0.0)
                    total[col, lev, :, 128 * who : 128 * (who + 1)] = kept[:8] + kept[8:]
        for at_level, lev in enumerate(levels):
            for col in range(COLUMNS):
                start = 16 * (COLUMNS * at_level + col)
                squares[col, lev] = norm[start : start + 8] + norm[start + 8 : start + 16]

    keep.wait()
    for copy in train_copies:
        copy.wait_recv()
    multiply([level] + [shifted(by) for by in NEAR])
    for row, source, on, which in far:
        for who in which:
            block = block_of(who, source - on)
            remote(block, block, far_send.at[row, who], far_recv.at[row, who], at(column, shifted(on)), group).wait_recv()
    multiply([shifted(by) for by in (3, 4, 5)])

    row = lax.broadcasted_iota(jnp.int32, (8, 128), 0)
    lane = lax.broadcasted_iota(jnp.int32, (8, 128), 1) // 32

    def fold(value):
        value = value + pltpu.roll(value, 64, 1)
        return value + pltpu.roll(value, 32, 1)

    per_column = ring // 2

    def make_tile(tile, carry):
        col, pair_of_levels = tile // per_column, lax.rem(tile, per_column)

        def rows_of(ref, lanes):
            even, odd = (ref[col, 2 * pair_of_levels + k, :, lanes] for k in range(2))
            even = even + pltpu.roll(even, 4, 0)
            odd = odd + pltpu.roll(odd, 4, 0)
            return jnp.where(row < 4, even, odd)

        value = fold(rows_of(total, slice(0, 128)))
        for who in range(1, COLUMNS):
            value = jnp.where(lane < who, value, fold(rows_of(total, slice(128 * who, 128 * (who + 1)))))
        norm = jnp.sum(rows_of(squares, slice(0, 128)), axis=1, keepdims=True)
        tiles[tile, :, :128] = value
        tiles[tile, :, 128:] = jnp.broadcast_to(norm, value.shape)
        return carry

    lax.fori_loop(0, tile_count, make_tile, 0)

    per_group = tile_count // groups

    def group_copy(d):
        to = lax.rem(group + d, groups)
        return remote(
            tiles.at[pl.ds(to * per_group, per_group)], tiles_in.at[d], r_send.at[d], r_recv.at[d], shard, to
        )

    def send_tile(d, carry):
        group_copy(d).start()
        return carry

    def add_tile(d, answer):
        group_copy(d).wait_recv()
        return answer + tiles_in[d]

    lax.fori_loop(1, groups, send_tile, 0)
    answer = lax.fori_loop(1, groups, add_tile, tiles[pl.ds(group * per_group, per_group)])
    summed[...] = answer
    pair_copies = []
    for who in (FIRST, SECOND, ACROSS):
        copy = remote(summed, summed_in.at[who], p_send.at[who], p_recv.at[who], at(columns[who], level), group)
        copy.start()
        pair_copies.append(copy)
    for copy in pair_copies:
        copy.wait_recv()
    raw, norm = answer[:, :, :32], answer[:, :, 128:129]
    for who in (FIRST, SECOND, ACROSS):
        raw = raw + summed_in[who, :, :, 32 * who : 32 * (who + 1)]
        norm = norm + summed_in[who, :, :, 128:129]
    out_ref[...] = (raw / jnp.sqrt(norm + EPSILON)).reshape(out_ref.shape)

    def tile_sent(d, carry):
        group_copy(d).wait_send()
        return carry

    lax.fori_loop(1, groups, tile_sent, 0)
    for copy in train_copies + column_copies + near_copies + far_copies + pair_copies:
        copy.wait_send()


def solution(mesh):
    shards, groups = mesh.shape["shard"], mesh.shape["layer"]
    ring = shards // COLUMNS

    def on_device(query_grads, out_basis, in_basis, eigen_scale, layer_slot, train_grads):
        local, slots, width = query_grads.shape
        side = out_basis.shape[1]
        rows = train_grads.shape[0]
        tile_count = local * shards // 8
        per_group = tile_count // groups
        dma = pltpu.SemaphoreType.DMA
        return pl.pallas_call(
            functools.partial(kernel, ring, groups),
            out_shape=jax.ShapeDtypeStruct((8 * per_group, rows), jnp.float32),
            in_specs=[pl.BlockSpec(memory_space=pl.ANY)] * 6,
            out_specs=pl.BlockSpec(memory_space=pltpu.VMEM),
            scratch_shapes=[
                pltpu.SMEM((slots,), jnp.int32),
                pltpu.VMEM((slots, local, width), jnp.bfloat16),
                pltpu.VMEM((slots, side, side), jnp.float32),
                pltpu.VMEM((slots, side, side), jnp.float32),
                pltpu.VMEM((slots, side, side), jnp.float32),
                pltpu.VMEM((slots, local * width // 128, 128), jnp.float32),
                pltpu.VMEM((slots, 2, local * width // 256, 128), jnp.float32),
                pltpu.VMEM((COLUMNS, 16, 256 * slots), jnp.bfloat16),
                pltpu.VMEM((COLUMNS, slots, rows, width // COLUMNS), jnp.bfloat16),
                pltpu.VMEM((COLUMNS, ring, 16, 256 * slots), jnp.bfloat16),
                pltpu.VMEM((COLUMNS, ring, 8, 128 * COLUMNS), jnp.float32),
                pltpu.VMEM((COLUMNS, ring, 8, 128), jnp.float32),
                pltpu.VMEM((tile_count, 8, 256), jnp.float32),
                pltpu.VMEM((groups, per_group, 8, 256), jnp.float32),
                pltpu.VMEM((per_group, 8, 256), jnp.float32),
                pltpu.VMEM((COLUMNS, per_group, 8, 256), jnp.float32),
                dma((6,)),
                dma((COLUMNS, 2)),
                dma((COLUMNS, 2)),
                dma((COLUMNS,)),
                dma((COLUMNS,)),
                dma((4, COLUMNS)),
                dma((4, COLUMNS)),
                dma((4, COLUMNS)),
                dma((4, COLUMNS)),
                dma((groups,)),
                dma((groups,)),
                dma((COLUMNS,)),
                dma((COLUMNS,)),
            ],
            compiler_params=pltpu.CompilerParams(
                collective_id=0, has_side_effects=True, vmem_limit_bytes=VMEM_BYTES
            ),
        )(
            layer_slot,
            jnp.transpose(query_grads, (1, 0, 2)),
            out_basis,
            in_basis,
            eigen_scale,
            jnp.transpose(train_grads, (1, 0, 2)),
        )

    return jax.shard_map(
        on_device,
        mesh=mesh,
        in_specs=(
            P("shard", "layer", None),
            P("layer", None, None),
            P("layer", None, None),
            P("layer", None, None),
            P("layer"),
            P("shard", "layer", None),
        ),
        out_specs=P("layer", "shard"),
        check_vma=False,
    )
```

```python
import functools

import jax
import jax.numpy as jnp
from jax import lax
from jax.experimental import pallas as pl
from jax.experimental.pallas import tpu as pltpu
from jax.sharding import PartitionSpec as P

DAMPING = 0.05
EPSILON = 1e-06
MESH = pl.DeviceIdType.MESH
PARTS = 8
COLUMNS = 4
OWN, FIRST, SECOND, ACROSS = range(4)
NEAR = (2, -2, 1, -1)
LOTS = (slice(0, 1), slice(1, 4), slice(0, 2), slice(2, 4))
VMEM_BYTES = 40 * 1024 * 1024


def split(value):
    top = value.astype(jnp.bfloat16)
    return top, (value - top.astype(jnp.float32)).astype(jnp.bfloat16)


def product(left, right, contract):
    dims = (contract, ((), ()))
    total = None
    for i, a in enumerate(left):
        for b in right[: len(right) - i]:
            term = lax.dot_general(a, b, dims, preferred_element_type=jnp.float32)
            total = term if total is None else total + term
    return total


def precondition_slot(index, slot, q_ref, s_ref, a_ref, e_ref, rows_ref, turned_ref, blocks_ref):
    side = s_ref.shape[1]
    width = q_ref.shape[2]
    pieces = width // 128
    half = side // 2
    queries = q_ref[index].astype(jnp.float32)
    for piece in range(pieces):
        rows_ref[slot, 4 * piece : 4 * piece + 4, :] = queries[:, 128 * piece : 128 * (piece + 1)]
    basis = jnp.concatenate([s_ref[index, pl.ds(parity, half, stride=2), :] for parity in range(2)], axis=0)
    right = split(a_ref[index])
    scale = e_ref[index] + DAMPING
    stacked = []
    for n in range(4):
        both = rows_ref[slot, pl.ds(n, half, stride=4), :]
        stacked.append(jnp.concatenate([both[:, :side], both[:, side:]], axis=0))
    stacked = jnp.concatenate(stacked, axis=0)
    stacked = product((stacked.astype(jnp.bfloat16),), right, ((1,), (0,)))
    wide = jnp.concatenate([stacked[side * n : side * (n + 1)] for n in range(4)], axis=1)
    wide = product(split(basis.T), split(wide), ((1,), (0,)))
    wide = wide / jnp.concatenate([scale] * 4, axis=1)
    wide = product(split(basis), split(wide), ((1,), (0,)))
    stacked = jnp.concatenate([wide[:, side * n : side * (n + 1)] for n in range(4)], axis=0)
    stacked = product(split(stacked), right, ((1,), (1,)))
    for n in range(4):
        block = stacked[side * n : side * (n + 1)]
        turned_ref[slot, pl.ds(n, half, stride=4), :] = jnp.concatenate([block[:half], block[half:]], axis=1)
    for part in range(PARTS):
        blocks_ref[part, :, 128 * slot : 128 * (slot + 1)] = turned_ref[slot, 16 * part : 16 * (part + 1), :].astype(
            jnp.bfloat16
        )


def kernel(
    ring,
    groups,
    slot_hbm,
    q_hbm,
    s_hbm,
    a_hbm,
    e_hbm,
    train_ref,
    out_ref,
    slot_ref,
    q_ref,
    s_ref,
    a_ref,
    e_ref,
    rows_ref,
    turned_ref,
    blocks_ref,
    train_part,
    gathered,
    tiles,
    tiles_in,
    pair_out,
    pair_in,
    local_sem,
    t_send,
    t_recv,
    q_send,
    q_recv,
    near_send,
    near_recv,
    far_send,
    far_recv,
    across_send,
    across_recv,
    r_send,
    r_recv,
    p_send,
    p_recv,
):
    shard = lax.axis_index("shard")
    group = lax.axis_index("layer")
    core = lax.rem(group, 2)
    column = shard // ring
    level = lax.rem(shard, ring)
    slots = q_ref.shape[0]
    tile_count = tiles.shape[0]

    def at(col, lev):
        return col * ring + lev

    def shifted(by):
        return lax.rem(level + by + ring, ring)

    first = column + 1 - 2 * lax.rem(column, 2)
    second = 3 - column
    across = 3 - first
    columns = [column, first, second, across]

    def remote(src, dst, send, recv, to_shard, to_group=group):
        return pltpu.make_async_remote_copy(
            src_ref=src, dst_ref=dst, send_sem=send, recv_sem=recv, device_id=(to_shard, to_group), device_id_type=MESH
        )

    barrier = pltpu.get_barrier_semaphore()
    partners = [(at(column, shifted(by)), group) for by in range(1, ring)]
    partners += [(at(c, level), group) for c in columns[1:]]
    for who in partners:
        pl.semaphore_signal(barrier, inc=1, device_id=who, device_id_type=MESH)

    def greet(d, carry):
        pl.semaphore_signal(barrier, inc=1, device_id=(shard, lax.rem(group + d, groups)), device_id_type=MESH)
        return carry

    lax.fori_loop(1, groups, greet, 0)
    loads = []
    for i, (src, dst) in enumerate(
        [(q_hbm, q_ref), (a_hbm, a_ref), (s_hbm, s_ref), (e_hbm, e_ref), (slot_hbm, slot_ref)]
    ):
        copy = pltpu.make_async_copy(src, dst, local_sem.at[i])
        copy.start()
        loads.append(copy)

    pl.semaphore_wait(barrier, len(partners) + groups - 1)

    span = train_ref.shape[2] // PARTS

    def part_of_train(part):
        return train_ref.at[:, :, pl.ds(pl.multiple_of(part * span, 128), span)]

    def train_to_column(who, half):
        i = 2 * who + half
        return remote(
            part_of_train(2 * columns[who] + half), train_part.at[i], t_send.at[i], t_recv.at[i], at(columns[who], level)
        )

    def train_to_level(i):
        to = shifted(-i)
        return remote(part_of_train(to), train_part.at[i], t_send.at[i], t_recv.at[i], at(column, to))

    def keep_for_column(half):
        return pltpu.make_async_copy(
            part_of_train(2 * column + half), train_part.at[half], local_sem.at[len(loads) + half]
        )

    def keep_for_level():
        return pltpu.make_async_copy(part_of_train(level), train_part.at[0], local_sem.at[len(loads)])

    @pl.when(core == 0)
    def _():
        for who in (FIRST, SECOND):
            train_to_column(who, 0).start()
        for half in range(2):
            keep_for_column(half).start()

    @pl.when(core == 1)
    def _():
        for i in (2, 6):
            train_to_level(i).start()
        keep_for_level().start()

    for copy in loads:
        copy.wait()
    for slot in range(slots):
        index = lax.rem(slot_ref[slot], slots)
        precondition_slot(index, slot, q_ref, s_ref, a_ref, e_ref, rows_ref, turned_ref, blocks_ref)

    @pl.when(core == 0)
    def _():
        def own_to_column(who):
            return remote(
                blocks_ref.at[pl.ds(2 * columns[who], 2)],
                gathered.at[:, who, level],
                q_send.at[who],
                q_recv.at[who],
                at(columns[who], level),
            )

        def block_of(lot, by):
            return gathered.at[:, LOTS[lot], shifted(by)]

        def near_copy(i, lot, source=0):
            block = block_of(lot, source)
            return remote(block, block, near_send.at[i, lot], near_recv.at[i, lot], at(column, shifted(NEAR[i])))

        for who in (FIRST, SECOND, ACROSS):
            own_to_column(who).start()
        for who in (FIRST, SECOND):
            train_to_column(who, 1).start()
        for half in range(2):
            gathered[half, OWN, level] = blocks_ref[2 * column + half]
        for i in range(len(NEAR)):
            near_copy(i, 0).start()
        for who in (FIRST, SECOND, ACROSS):
            own_to_column(who).wait_recv()
        for i in range(len(NEAR)):
            near_copy(i, 1).start()
        for half in range(2):
            train_to_column(ACROSS, half).start()

        def far_copy(row, lot, source, on):
            block = block_of(lot, source)
            return remote(block, block, far_send.at[row, lot], far_recv.at[row, lot], at(column, shifted(on)))

        far = [(0, 0, -2, 1), (1, 0, 2, -1), (0, 1, -2, 1), (1, 1, 2, -1), (2, 2, -2, 2), (3, 3, 2, -2)]
        for lot in range(2):
            for i in range(2):
                near_copy(i, lot, -NEAR[i]).wait_recv()
        for row, lot, source, on in far:
            far_copy(row, lot, source, on).start()
        for lot in range(2):
            for i in range(2, len(NEAR)):
                near_copy(i, lot, -NEAR[i]).wait_recv()
        for row, lot, source, on in far:
            far_copy(row, lot, source - on, on).wait_recv()
        for half in range(2):
            keep_for_column(half).wait()
            for who in (FIRST, SECOND, ACROSS):
                train_to_column(who, half).wait_recv()
        for half in range(2):
            for who in (FIRST, SECOND, ACROSS):
                train_to_column(who, half).wait_send()
        for who in (FIRST, SECOND, ACROSS):
            own_to_column(who).wait_send()
        for lot in range(2):
            for i in range(len(NEAR)):
                near_copy(i, lot).wait_send()
        for row, lot, source, on in far:
            far_copy(row, lot, source, on).wait_send()

    @pl.when(core == 1)
    def _():
        def own_to_level(i):
            to = shifted(-i)
            return remote(
                blocks_ref.at[to], gathered.at[0, OWN, level], q_send.at[i], q_recv.at[i], at(column, to)
            )

        def levels_to_column(who):
            return remote(
                gathered.at[0, OWN],
                gathered.at[0, who],
                across_send.at[who],
                across_recv.at[who],
                at(columns[who], level),
            )

        order = (4, 3, 5, 2, 6, 1, 7)
        for i in order:
            own_to_level(i).start()
        for i in (1, 7, 3, 5, 4):
            train_to_level(i).start()
        gathered[0, OWN, level] = blocks_ref[level]
        for i in order:
            remote(
                blocks_ref.at[0],
                gathered.at[0, OWN, shifted(i)],
                q_send.at[i],
                q_recv.at[i],
                at(column, shifted(-i)),
            ).wait_recv()
        for who in (ACROSS, FIRST, SECOND):
            levels_to_column(who).start()
        for who in (ACROSS, FIRST, SECOND):
            levels_to_column(who).wait_recv()
        keep_for_level().wait()
        for i in range(1, ring):
            train_to_level(i).wait_recv()
        for i in range(1, ring):
            train_to_level(i).wait_send()
            own_to_level(i).wait_send()
        for who in (ACROSS, FIRST, SECOND):
            levels_to_column(who).wait_send()

    count = COLUMNS * ring
    left = [gathered[part].reshape(16 * count, 128 * slots) for part in (0, 1 - core)]
    squares = [value.astype(jnp.float32) for value in left]
    squares = squares[0] * squares[0] + jnp.where(core == 0, squares[1] * squares[1], 0.0)
    norm = squares[:, :128]
    for slot in range(1, slots):
        norm = norm + squares[:, 128 * slot : 128 * (slot + 1)]

    row = lax.broadcasted_iota(jnp.int32, (tile_count, 8, 128), 1)
    lane = lax.broadcasted_iota(jnp.int32, (tile_count, 8, 128), 2) // 32
    same = lax.broadcasted_iota(jnp.int32, (count, 16, 128), 1) // 4 == (
        lax.broadcasted_iota(jnp.int32, (count, 16, 128), 2) // 32
    )

    def queries_of(value):
        value = value[:, :8] + value[:, 8:]
        value = (value + pltpu.roll(value, 4, 1)).reshape(tile_count, 2, 8, 128)
        return jnp.where(row < 4, value[:, 0], value[:, 1])

    low = jnp.zeros((tile_count, 8, 128), jnp.float32)
    high = low
    for i in range(PARTS):
        right = jnp.concatenate(
            [
                jnp.concatenate([train_part[i, slot, :, 128 * sub : 128 * (sub + 1)] for slot in range(slots)], axis=1)
                for sub in range(4)
            ],
            axis=0,
        )
        product = lax.dot_general(
            left[i % 2], right, (((1,), (1,)), ((), ())), preferred_element_type=jnp.float32
        ).reshape(count, 16, 128)
        value = queries_of(jnp.where(same, product, 0.0))
        value = value + pltpu.roll(value, 64, 2)
        value = value + pltpu.roll(value, 32, 2)
        low = low + jnp.where(lane == jnp.where(core == 0, i // 2, i), value, 0.0)
        if i >= 4:
            high = high + jnp.where(lane == i - 4, value, 0.0)
    norm = jnp.sum(queries_of(norm.reshape(count, 16, 128)), axis=2, keepdims=True)
    per_column = tile_count // COLUMNS
    for who in range(COLUMNS):
        place = pl.ds(columns[who] * per_column, per_column)
        some = slice(who * per_column, (who + 1) * per_column)
        tiles[place, :, :128] = low[some]
        tiles[place, :, 128:256] = high[some]
        tiles[place, :, 256:] = jnp.broadcast_to(norm[some], (per_column, 8, 128))

    per_group = tile_count // groups

    def group_copy(d):
        to = lax.rem(group + d, groups)
        return remote(
            tiles.at[pl.ds(to * per_group, per_group)], tiles_in.at[d], r_send.at[d], r_recv.at[d], shard, to
        )

    def send_tile(d, carry):
        group_copy(d).start()
        return carry

    lax.fori_loop(1, groups, send_tile, 0)
    sums = [tiles[pl.ds(group * per_group, per_group)], None]
    for d in range(1, groups):
        group_copy(d).wait_recv()
        sums[d % 2] = tiles_in[d] if sums[d % 2] is None else sums[d % 2] + tiles_in[d]
    by_column = jnp.where(core == 0, sums[0], sums[1])
    by_level = jnp.where(core == 0, sums[1], sums[0])

    scores_of = [by_column[:, :, :128]] * COLUMNS + [by_level[:, :, :128]] * 4 + [by_level[:, :, 128:256]] * 4
    squares_of = [by_column[:, :, 256:]] * COLUMNS + [by_level[:, :, 256:]] * ring
    is_score = lax.broadcasted_iota(jnp.int32, (per_group, 8, 128), 2) < 32

    def packed(j):
        turned = scores_of[j] if j % 4 == 0 else pltpu.roll(scores_of[j], 128 - 32 * (j % 4), 2)
        return jnp.where(is_score, turned, squares_of[j])

    def pair_copy(j):
        to = at(columns[j], level) if j < COLUMNS else at(column, shifted(j - COLUMNS))
        return remote(pair_out.at[j], pair_in.at[j], p_send.at[j], p_recv.at[j], to)

    others = [COLUMNS + i for i in (4, 3, 5)] + [ACROSS] + [COLUMNS + i for i in (2, 6)] + [FIRST, SECOND]
    others += [COLUMNS + i for i in (1, 7)]
    for j in others:
        pair_out[j] = packed(j)
        pair_copy(j).start()
    answer = packed(OWN) + packed(COLUMNS)
    for j in reversed(others):
        pair_copy(j).wait_recv()
        answer = answer + pair_in[j]
    out_ref[...] = (answer[:, :, :32] / jnp.sqrt(answer[:, :, 32:33] + EPSILON)).reshape(out_ref.shape)

    def tile_sent(d, carry):
        group_copy(d).wait_send()
        return carry

    lax.fori_loop(1, groups, tile_sent, 0)
    for j in others:
        pair_copy(j).wait_send()


def solution(mesh):
    shards, groups = mesh.shape["shard"], mesh.shape["layer"]
    ring = shards // COLUMNS

    def on_device(query_grads, out_basis, in_basis, eigen_scale, layer_slot, train_grads):
        local, slots, width = query_grads.shape
        side = out_basis.shape[1]
        rows = train_grads.shape[0]
        tile_count = local * shards // 8
        per_group = tile_count // groups
        dma = pltpu.SemaphoreType.DMA
        return pl.pallas_call(
            functools.partial(kernel, ring, groups),
            out_shape=jax.ShapeDtypeStruct((8 * per_group, rows), jnp.float32),
            in_specs=[pl.BlockSpec(memory_space=pl.ANY)] * 6,
            out_specs=pl.BlockSpec(memory_space=pltpu.VMEM),
            scratch_shapes=[
                pltpu.SMEM((slots,), jnp.int32),
                pltpu.VMEM((slots, local, width), jnp.bfloat16),
                pltpu.VMEM((slots, side, side), jnp.float32),
                pltpu.VMEM((slots, side, side), jnp.float32),
                pltpu.VMEM((slots, side, side), jnp.float32),
                pltpu.VMEM((slots, local * width // 128, 128), jnp.float32),
                pltpu.VMEM((slots, local * width // 128, 128), jnp.float32),
                pltpu.VMEM((PARTS, 16, 128 * slots), jnp.bfloat16),
                pltpu.VMEM((PARTS, slots, rows, width // PARTS), jnp.bfloat16),
                pltpu.VMEM((2, COLUMNS, ring, 16, 128 * slots), jnp.bfloat16),
                pltpu.VMEM((tile_count, 8, 384), jnp.float32),
                pltpu.VMEM((groups, per_group, 8, 384), jnp.float32),
                pltpu.VMEM((COLUMNS + ring, per_group, 8, 128), jnp.float32),
                pltpu.VMEM((COLUMNS + ring, per_group, 8, 128), jnp.float32),
                dma((7,)),
                dma((PARTS,)),
                dma((PARTS,)),
                dma((ring,)),
                dma((ring,)),
                dma((len(NEAR), 2)),
                dma((len(NEAR), 2)),
                dma((4, 4)),
                dma((4, 4)),
                dma((COLUMNS,)),
                dma((COLUMNS,)),
                dma((groups,)),
                dma((groups,)),
                dma((COLUMNS + ring,)),
                dma((COLUMNS + ring,)),
            ],
            compiler_params=pltpu.CompilerParams(
                collective_id=0, has_side_effects=True, vmem_limit_bytes=VMEM_BYTES
            ),
        )(
            *[
                pltpu.with_memory_space_constraint(x, pltpu.HBM)
                for x in (
                    layer_slot,
                    jnp.transpose(query_grads, (1, 0, 2)),
                    out_basis,
                    in_basis,
                    eigen_scale,
                    jnp.transpose(train_grads, (1, 0, 2)),
                )
            ]
        )

    return jax.shard_map(
        on_device,
        mesh=mesh,
        in_specs=(
            P("shard", "layer", None),
            P("layer", None, None),
            P("layer", None, None),
            P("layer", None, None),
            P("layer"),
            P("shard", "layer", None),
        ),
        out_specs=P("layer", "shard"),
        check_vma=False,
    )
```

```python
import functools

import jax
import jax.numpy as jnp
from jax import lax
from jax.experimental import pallas as pl
from jax.experimental.pallas import tpu as pltpu
from jax.sharding import PartitionSpec as P

DAMPING = 0.05
EPSILON = 1e-06
MESH = pl.DeviceIdType.MESH
PARTS = 8
COLUMNS = 4
OWN, FIRST, SECOND, ACROSS = range(4)
NEAR = (2, -2, 1, -1)
LOTS = (slice(0, 1), slice(1, 4), slice(0, 2), slice(2, 4))
VMEM_BYTES = 40 * 1024 * 1024


def split(value):
    top = value.astype(jnp.bfloat16)
    return top, (value - top.astype(jnp.float32)).astype(jnp.bfloat16)


def product(left, right, contract):
    dims = (contract, ((), ()))
    total = None
    for i, a in enumerate(left):
        for b in right[: len(right) - i]:
            term = lax.dot_general(a, b, dims, preferred_element_type=jnp.float32)
            total = term if total is None else total + term
    return total


def precondition_slot(index, slot, q_ref, s_ref, a_ref, e_ref, rows_ref, turned_ref, blocks_ref):
    side = s_ref.shape[1]
    width = q_ref.shape[2]
    pieces = width // 128
    half = side // 2
    queries = q_ref[index].astype(jnp.float32)
    for piece in range(pieces):
        rows_ref[slot, 4 * piece : 4 * piece + 4, :] = queries[:, 128 * piece : 128 * (piece + 1)]
    basis = jnp.concatenate([s_ref[index, pl.ds(parity, half, stride=2), :] for parity in range(2)], axis=0)
    right = split(a_ref[index])
    scale = e_ref[index] + DAMPING
    stacked = []
    for n in range(4):
        both = rows_ref[slot, pl.ds(n, half, stride=4), :]
        stacked.append(jnp.concatenate([both[:, :side], both[:, side:]], axis=0))
    stacked = jnp.concatenate(stacked, axis=0)
    stacked = product((stacked.astype(jnp.bfloat16),), right, ((1,), (0,)))
    wide = jnp.concatenate([stacked[side * n : side * (n + 1)] for n in range(4)], axis=1)
    wide = product(split(basis.T), split(wide), ((1,), (0,)))
    wide = wide / jnp.concatenate([scale] * 4, axis=1)
    wide = product(split(basis), split(wide), ((1,), (0,)))
    stacked = jnp.concatenate([wide[:, side * n : side * (n + 1)] for n in range(4)], axis=0)
    stacked = product(split(stacked), right, ((1,), (1,)))
    for n in range(4):
        block = stacked[side * n : side * (n + 1)]
        turned_ref[slot, pl.ds(n, half, stride=4), :] = jnp.concatenate([block[:half], block[half:]], axis=1)
    for part in range(PARTS):
        blocks_ref[part, :, 128 * slot : 128 * (slot + 1)] = turned_ref[slot, 16 * part : 16 * (part + 1), :].astype(
            jnp.bfloat16
        )


def kernel(
    ring,
    groups,
    slot_hbm,
    q_hbm,
    s_hbm,
    a_hbm,
    e_hbm,
    train_ref,
    out_ref,
    slot_ref,
    q_ref,
    s_ref,
    a_ref,
    e_ref,
    rows_ref,
    turned_ref,
    blocks_ref,
    train_part,
    gathered,
    tiles,
    tiles_in,
    pair_out,
    pair_in,
    local_sem,
    t_send,
    t_recv,
    q_send,
    q_recv,
    near_send,
    near_recv,
    far_send,
    far_recv,
    across_send,
    across_recv,
    r_send,
    r_recv,
    p_send,
    p_recv,
):
    shard = lax.axis_index("shard")
    group = lax.axis_index("layer")
    core = lax.rem(group, 2)
    column = shard // ring
    level = lax.rem(shard, ring)
    slots = q_ref.shape[0]
    tile_count = tiles.shape[0]

    def at(col, lev):
        return col * ring + lev

    def shifted(by):
        return lax.rem(level + by + ring, ring)

    first = column + 1 - 2 * lax.rem(column, 2)
    second = 3 - column
    across = 3 - first
    columns = [column, first, second, across]

    def remote(src, dst, send, recv, to_shard, to_group=group):
        return pltpu.make_async_remote_copy(
            src_ref=src, dst_ref=dst, send_sem=send, recv_sem=recv, device_id=(to_shard, to_group), device_id_type=MESH
        )

    loads = []
    for i, (src, dst) in enumerate(
        [(q_hbm, q_ref), (a_hbm, a_ref), (s_hbm, s_ref), (e_hbm, e_ref), (slot_hbm, slot_ref)]
    ):
        copy = pltpu.make_async_copy(src, dst, local_sem.at[i])
        copy.start()
        loads.append(copy)


    barrier = pltpu.get_barrier_semaphore()
    partners = [(at(column, shifted(by)), group) for by in range(1, ring)]
    partners += [(at(c, level), group) for c in columns[1:]]
    for who in partners:
        pl.semaphore_signal(barrier, inc=1, device_id=who, device_id_type=MESH)

    def greet(d, carry):
        pl.semaphore_signal(barrier, inc=1, device_id=(shard, lax.rem(group + d, groups)), device_id_type=MESH)
        return carry

    lax.fori_loop(1, groups, greet, 0)
    span = train_ref.shape[2] // PARTS

    def part_of_train(part):
        return train_ref.at[:, :, pl.ds(pl.multiple_of(part * span, 128), span)]

    def train_to_column(who, half):
        i = 2 * who + half
        return remote(
            part_of_train(2 * columns[who] + half), train_part.at[i], t_send.at[i], t_recv.at[i], at(columns[who], level)
        )

    def train_to_level(i):
        to = shifted(-i)
        return remote(part_of_train(to), train_part.at[i], t_send.at[i], t_recv.at[i], at(column, to))

    def keep_for_column(half):
        return pltpu.make_async_copy(
            part_of_train(2 * column + half), train_part.at[half], local_sem.at[len(loads) + half]
        )

    def keep_for_level():
        return pltpu.make_async_copy(part_of_train(level), train_part.at[0], local_sem.at[len(loads)])

    @pl.when(core == 0)
    def _():
        for half in range(2):
            keep_for_column(half).start()

    @pl.when(core == 1)
    def _():
        keep_for_level().start()

    for copy in loads:
        copy.wait()
    for slot in range(slots):
        index = lax.rem(slot_ref[slot], slots)
        precondition_slot(index, slot, q_ref, s_ref, a_ref, e_ref, rows_ref, turned_ref, blocks_ref)

    pl.semaphore_wait(barrier, len(partners) + groups - 1)

    @pl.when(core == 0)
    def _():
        def own_to_column(who):
            return remote(
                blocks_ref.at[pl.ds(2 * columns[who], 2)],
                gathered.at[:, who, level],
                q_send.at[who],
                q_recv.at[who],
                at(columns[who], level),
            )

        def block_of(lot, by):
            return gathered.at[:, LOTS[lot], shifted(by)]

        def near_copy(i, lot, source=0):
            block = block_of(lot, source)
            return remote(block, block, near_send.at[i, lot], near_recv.at[i, lot], at(column, shifted(NEAR[i])))

        for who in (FIRST, SECOND, ACROSS):
            own_to_column(who).start()
        for half in range(2):
            gathered[half, OWN, level] = blocks_ref[2 * column + half]
        for i in range(len(NEAR)):
            near_copy(i, 0).start()
        for who in (FIRST, SECOND):
            train_to_column(who, 0).start()
        for who in (FIRST, SECOND):
            train_to_column(who, 1).start()
        for who in (FIRST, SECOND, ACROSS):
            own_to_column(who).wait_recv()
        for i in range(len(NEAR)):
            near_copy(i, 1).start()
        for half in range(2):
            train_to_column(ACROSS, half).start()

        def far_copy(row, lot, source, on):
            block = block_of(lot, source)
            return remote(block, block, far_send.at[row, lot], far_recv.at[row, lot], at(column, shifted(on)))

        far = [(0, 0, -2, 1), (1, 0, 2, -1), (0, 1, -2, 1), (1, 1, 2, -1), (2, 2, -2, 2), (3, 3, 2, -2)]
        for lot in range(2):
            for i in range(2):
                near_copy(i, lot, -NEAR[i]).wait_recv()
        for row, lot, source, on in far:
            far_copy(row, lot, source, on).start()
        for lot in range(2):
            for i in range(2, len(NEAR)):
                near_copy(i, lot, -NEAR[i]).wait_recv()
        for row, lot, source, on in far:
            far_copy(row, lot, source - on, on).wait_recv()
        for half in range(2):
            keep_for_column(half).wait()
            for who in (FIRST, SECOND, ACROSS):
                train_to_column(who, half).wait_recv()
        for half in range(2):
            for who in (FIRST, SECOND, ACROSS):
                train_to_column(who, half).wait_send()
        for who in (FIRST, SECOND, ACROSS):
            own_to_column(who).wait_send()
        for lot in range(2):
            for i in range(len(NEAR)):
                near_copy(i, lot).wait_send()
        for row, lot, source, on in far:
            far_copy(row, lot, source, on).wait_send()

    @pl.when(core == 1)
    def _():
        def own_to_level(i):
            to = shifted(-i)
            return remote(
                blocks_ref.at[to], gathered.at[0, OWN, level], q_send.at[i], q_recv.at[i], at(column, to)
            )

        def levels_to_column(who):
            return remote(
                gathered.at[0, OWN],
                gathered.at[0, who],
                across_send.at[who],
                across_recv.at[who],
                at(columns[who], level),
            )

        order = (4, 3, 5, 2, 6, 1, 7)
        for i in order:
            own_to_level(i).start()
        for i in (2, 6, 1, 7, 3, 5, 4):
            train_to_level(i).start()
        gathered[0, OWN, level] = blocks_ref[level]
        for i in order:
            remote(
                blocks_ref.at[0],
                gathered.at[0, OWN, shifted(i)],
                q_send.at[i],
                q_recv.at[i],
                at(column, shifted(-i)),
            ).wait_recv()
        for who in (ACROSS, FIRST, SECOND):
            levels_to_column(who).start()
        for who in (ACROSS, FIRST, SECOND):
            levels_to_column(who).wait_recv()
        keep_for_level().wait()
        for i in range(1, ring):
            train_to_level(i).wait_recv()
        for i in range(1, ring):
            train_to_level(i).wait_send()
            own_to_level(i).wait_send()
        for who in (ACROSS, FIRST, SECOND):
            levels_to_column(who).wait_send()

    count = COLUMNS * ring
    left = [gathered[part].reshape(16 * count, 128 * slots) for part in (0, 1 - core)]
    squares = [value.astype(jnp.float32) for value in left]
    squares = squares[0] * squares[0] + jnp.where(core == 0, squares[1] * squares[1], 0.0)
    norm = squares[:, :128]
    for slot in range(1, slots):
        norm = norm + squares[:, 128 * slot : 128 * (slot + 1)]

    row = lax.broadcasted_iota(jnp.int32, (tile_count, 8, 128), 1)
    lane = lax.broadcasted_iota(jnp.int32, (tile_count, 8, 128), 2) // 32
    same = lax.broadcasted_iota(jnp.int32, (count, 16, 128), 1) // 4 == (
        lax.broadcasted_iota(jnp.int32, (count, 16, 128), 2) // 32
    )

    def queries_of(value):
        value = value[:, :8] + value[:, 8:]
        value = (value + pltpu.roll(value, 4, 1)).reshape(tile_count, 2, 8, 128)
        return jnp.where(row < 4, value[:, 0], value[:, 1])

    low = jnp.zeros((tile_count, 8, 128), jnp.float32)
    high = low
    for i in range(PARTS):
        right = jnp.concatenate(
            [
                jnp.concatenate([train_part[i, slot, :, 128 * sub : 128 * (sub + 1)] for slot in range(slots)], axis=1)
                for sub in range(4)
            ],
            axis=0,
        )
        product = lax.dot_general(
            left[i % 2], right, (((1,), (1,)), ((), ())), preferred_element_type=jnp.float32
        ).reshape(count, 16, 128)
        value = queries_of(jnp.where(same, product, 0.0))
        value = value + pltpu.roll(value, 64, 2)
        value = value + pltpu.roll(value, 32, 2)
        low = low + jnp.where(lane == jnp.where(core == 0, i // 2, i), value, 0.0)
        if i >= 4:
            high = high + jnp.where(lane == i - 4, value, 0.0)
    norm = jnp.sum(queries_of(norm.reshape(count, 16, 128)), axis=2, keepdims=True)
    per_column = tile_count // COLUMNS
    for who in range(COLUMNS):
        place = pl.ds(columns[who] * per_column, per_column)
        some = slice(who * per_column, (who + 1) * per_column)
        tiles[place, :, :128] = low[some]
        tiles[place, :, 128:256] = high[some]
        tiles[place, :, 256:] = jnp.broadcast_to(norm[some], (per_column, 8, 128))

    per_group = tile_count // groups

    def group_copy(d):
        to = lax.rem(group + d, groups)
        return remote(
            tiles.at[pl.ds(to * per_group, per_group)], tiles_in.at[d], r_send.at[d], r_recv.at[d], shard, to
        )

    for d in sorted(range(1, groups), key=lambda d: abs(2 * d - groups)):
        group_copy(d).start()
    sums = [tiles[pl.ds(group * per_group, per_group)], None]
    for d in range(1, groups):
        group_copy(d).wait_recv()
        sums[d % 2] = tiles_in[d] if sums[d % 2] is None else sums[d % 2] + tiles_in[d]
    by_column = jnp.where(core == 0, sums[0], sums[1])
    by_level = jnp.where(core == 0, sums[1], sums[0])

    scores_of = [by_column[:, :, :128]] * COLUMNS + [by_level[:, :, :128]] * 4 + [by_level[:, :, 128:256]] * 4
    squares_of = [by_column[:, :, 256:]] * COLUMNS + [by_level[:, :, 256:]] * ring
    is_score = lax.broadcasted_iota(jnp.int32, (per_group, 8, 128), 2) < 32

    def packed(j):
        turned = scores_of[j] if j % 4 == 0 else pltpu.roll(scores_of[j], 128 - 32 * (j % 4), 2)
        return jnp.where(is_score, turned, squares_of[j])

    def pair_copy(j):
        to = at(columns[j], level) if j < COLUMNS else at(column, shifted(j - COLUMNS))
        return remote(pair_out.at[j], pair_in.at[j], p_send.at[j], p_recv.at[j], to)

    others = [COLUMNS + i for i in (4, 3, 5)] + [ACROSS] + [COLUMNS + i for i in (2, 6)] + [FIRST, SECOND]
    others += [COLUMNS + i for i in (1, 7)]
    for j in others:
        pair_out[j] = packed(j)
        pair_copy(j).start()
    answer = packed(OWN) + packed(COLUMNS)
    for j in reversed(others):
        pair_copy(j).wait_recv()
        answer = answer + pair_in[j]
    out_ref[...] = (answer[:, :, :32] / jnp.sqrt(answer[:, :, 32:33] + EPSILON)).reshape(out_ref.shape)

    def tile_sent(d, carry):
        group_copy(d).wait_send()
        return carry

    lax.fori_loop(1, groups, tile_sent, 0)
    for j in others:
        pair_copy(j).wait_send()


def solution(mesh):
    shards, groups = mesh.shape["shard"], mesh.shape["layer"]
    ring = shards // COLUMNS

    def on_device(query_grads, out_basis, in_basis, eigen_scale, layer_slot, train_grads):
        local, slots, width = query_grads.shape
        side = out_basis.shape[1]
        rows = train_grads.shape[0]
        tile_count = local * shards // 8
        per_group = tile_count // groups
        dma = pltpu.SemaphoreType.DMA
        return pl.pallas_call(
            functools.partial(kernel, ring, groups),
            out_shape=jax.ShapeDtypeStruct((8 * per_group, rows), jnp.float32),
            in_specs=[pl.BlockSpec(memory_space=pl.ANY)] * 6,
            out_specs=pl.BlockSpec(memory_space=pltpu.VMEM),
            scratch_shapes=[
                pltpu.SMEM((slots,), jnp.int32),
                pltpu.VMEM((slots, local, width), jnp.bfloat16),
                pltpu.VMEM((slots, side, side), jnp.float32),
                pltpu.VMEM((slots, side, side), jnp.float32),
                pltpu.VMEM((slots, side, side), jnp.float32),
                pltpu.VMEM((slots, local * width // 128, 128), jnp.float32),
                pltpu.VMEM((slots, local * width // 128, 128), jnp.float32),
                pltpu.VMEM((PARTS, 16, 128 * slots), jnp.bfloat16),
                pltpu.VMEM((PARTS, slots, rows, width // PARTS), jnp.bfloat16),
                pltpu.VMEM((2, COLUMNS, ring, 16, 128 * slots), jnp.bfloat16),
                pltpu.VMEM((tile_count, 8, 384), jnp.float32),
                pltpu.VMEM((groups, per_group, 8, 384), jnp.float32),
                pltpu.VMEM((COLUMNS + ring, per_group, 8, 128), jnp.float32),
                pltpu.VMEM((COLUMNS + ring, per_group, 8, 128), jnp.float32),
                dma((7,)),
                dma((PARTS,)),
                dma((PARTS,)),
                dma((ring,)),
                dma((ring,)),
                dma((len(NEAR), 2)),
                dma((len(NEAR), 2)),
                dma((4, 4)),
                dma((4, 4)),
                dma((COLUMNS,)),
                dma((COLUMNS,)),
                dma((groups,)),
                dma((groups,)),
                dma((COLUMNS + ring,)),
                dma((COLUMNS + ring,)),
            ],
            compiler_params=pltpu.CompilerParams(
                collective_id=0, has_side_effects=True, vmem_limit_bytes=VMEM_BYTES
            ),
        )(
            *[
                pltpu.with_memory_space_constraint(x, pltpu.HBM)
                for x in (
                    layer_slot,
                    jnp.transpose(query_grads, (1, 0, 2)),
                    out_basis,
                    in_basis,
                    eigen_scale,
                    jnp.transpose(train_grads, (1, 0, 2)),
                )
            ]
        )

    return jax.shard_map(
        on_device,
        mesh=mesh,
        in_specs=(
            P("shard", "layer", None),
            P("layer", None, None),
            P("layer", None, None),
            P("layer", None, None),
            P("layer"),
            P("shard", "layer", None),
        ),
        out_specs=P("layer", "shard"),
        check_vma=False,
    )
```

```python
import functools

import jax
import jax.numpy as jnp
from jax import lax
from jax.experimental import pallas as pl
from jax.experimental.pallas import tpu as pltpu
from jax.sharding import PartitionSpec as P

DAMPING = 0.05
EPSILON = 1e-06
MESH = pl.DeviceIdType.MESH
PARTS = 8
COLUMNS = 4
OWN, FIRST, SECOND, ACROSS = range(4)
NEAR = (2, -2, 1, -1)
LOTS = (slice(0, 1), slice(1, 3), slice(3, 4), slice(0, 2), slice(2, 4))
VMEM_BYTES = 40 * 1024 * 1024


def split(value):
    top = value.astype(jnp.bfloat16)
    return top, (value - top.astype(jnp.float32)).astype(jnp.bfloat16)


def product(left, right, contract):
    dims = (contract, ((), ()))
    total = None
    for i, a in enumerate(left):
        for b in right[: len(right) - i]:
            term = lax.dot_general(a, b, dims, preferred_element_type=jnp.float32)
            total = term if total is None else total + term
    return total


def precondition_slot(index, slot, q_ref, s_ref, a_ref, e_ref, rows_ref, turned_ref, blocks_ref):
    side = s_ref.shape[1]
    width = q_ref.shape[2]
    pieces = width // 128
    half = side // 2
    queries = q_ref[index].astype(jnp.float32)
    for piece in range(pieces):
        rows_ref[slot, 4 * piece : 4 * piece + 4, :] = queries[:, 128 * piece : 128 * (piece + 1)]
    basis = jnp.concatenate([s_ref[index, pl.ds(parity, half, stride=2), :] for parity in range(2)], axis=0)
    right = split(a_ref[index])
    scale = e_ref[index] + DAMPING
    stacked = []
    for n in range(4):
        both = rows_ref[slot, pl.ds(n, half, stride=4), :]
        stacked.append(jnp.concatenate([both[:, :side], both[:, side:]], axis=0))
    stacked = jnp.concatenate(stacked, axis=0)
    stacked = product((stacked.astype(jnp.bfloat16),), right, ((1,), (0,)))
    wide = jnp.concatenate([stacked[side * n : side * (n + 1)] for n in range(4)], axis=1)
    wide = product(split(basis.T), split(wide), ((1,), (0,)))
    wide = wide / jnp.concatenate([scale] * 4, axis=1)
    wide = product(split(basis), split(wide), ((1,), (0,)))
    stacked = jnp.concatenate([wide[:, side * n : side * (n + 1)] for n in range(4)], axis=0)
    stacked = product(split(stacked), right, ((1,), (1,)))
    for n in range(4):
        block = stacked[side * n : side * (n + 1)]
        turned_ref[slot, pl.ds(n, half, stride=4), :] = jnp.concatenate([block[:half], block[half:]], axis=1)
    for part in range(PARTS):
        blocks_ref[part, :, 128 * slot : 128 * (slot + 1)] = turned_ref[slot, 16 * part : 16 * (part + 1), :].astype(
            jnp.bfloat16
        )


def kernel(
    ring,
    groups,
    slot_hbm,
    q_hbm,
    s_hbm,
    a_hbm,
    e_hbm,
    train_ref,
    out_ref,
    slot_ref,
    q_ref,
    s_ref,
    a_ref,
    e_ref,
    rows_ref,
    turned_ref,
    blocks_ref,
    train_part,
    gathered,
    scored,
    tiles,
    tiles_in,
    pair_out,
    pair_in,
    local_sem,
    t_send,
    t_recv,
    q_send,
    q_recv,
    near_send,
    near_recv,
    far_send,
    far_recv,
    across_send,
    across_recv,
    r_send,
    r_recv,
    p_send,
    p_recv,
):
    shard = lax.axis_index("shard")
    group = lax.axis_index("layer")
    core = lax.rem(group, 2)
    column = shard // ring
    level = lax.rem(shard, ring)
    slots = q_ref.shape[0]
    tile_count = tiles.shape[0]

    def at(col, lev):
        return col * ring + lev

    def shifted(by):
        return lax.rem(level + by + ring, ring)

    first = column + 1 - 2 * lax.rem(column, 2)
    second = 3 - column
    across = 3 - first
    columns = [column, first, second, across]

    def remote(src, dst, send, recv, to_shard, to_group=group):
        return pltpu.make_async_remote_copy(
            src_ref=src, dst_ref=dst, send_sem=send, recv_sem=recv, device_id=(to_shard, to_group), device_id_type=MESH
        )

    loads = []
    for i, (src, dst) in enumerate(
        [(q_hbm, q_ref), (a_hbm, a_ref), (s_hbm, s_ref), (e_hbm, e_ref), (slot_hbm, slot_ref)]
    ):
        copy = pltpu.make_async_copy(src, dst, local_sem.at[i])
        copy.start()
        loads.append(copy)


    barrier = pltpu.get_barrier_semaphore()
    partners = [(at(column, shifted(by)), group) for by in range(1, ring)]
    partners += [(at(c, level), group) for c in columns[1:]]
    for who in partners:
        pl.semaphore_signal(barrier, inc=1, device_id=who, device_id_type=MESH)

    def greet(d, carry):
        pl.semaphore_signal(barrier, inc=1, device_id=(shard, lax.rem(group + d, groups)), device_id_type=MESH)
        return carry

    lax.fori_loop(1, groups, greet, 0)
    span = train_ref.shape[2] // PARTS

    def part_of_train(part):
        return train_ref.at[:, :, pl.ds(pl.multiple_of(part * span, 128), span)]

    def train_to_column(who, half):
        i = 2 * who + half
        return remote(
            part_of_train(2 * columns[who] + half), train_part.at[i], t_send.at[i], t_recv.at[i], at(columns[who], level)
        )

    def train_to_level(i):
        to = shifted(-i)
        return remote(part_of_train(to), train_part.at[i], t_send.at[i], t_recv.at[i], at(column, to))

    def keep_for_column(half):
        return pltpu.make_async_copy(
            part_of_train(2 * column + half), train_part.at[half], local_sem.at[len(loads) + half]
        )

    def keep_for_level():
        return pltpu.make_async_copy(part_of_train(level), train_part.at[0], local_sem.at[len(loads)])

    @pl.when(core == 0)
    def _():
        for half in range(2):
            keep_for_column(half).start()

    @pl.when(core == 1)
    def _():
        keep_for_level().start()

    for copy in loads:
        copy.wait()
    for slot in range(slots):
        index = lax.rem(slot_ref[slot], slots)
        precondition_slot(index, slot, q_ref, s_ref, a_ref, e_ref, rows_ref, turned_ref, blocks_ref)

    pl.semaphore_wait(barrier, len(partners) + groups - 1)

    def score(whos, levels):
        many = whos.stop - whos.start
        count = many * len(levels)

        def blocks_of(part):
            value = [gathered[part, whos, pl.ds(lev, 1)].reshape(16 * many, 128 * slots) for lev in levels]
            return jnp.concatenate(value, axis=0) if len(value) > 1 else value[0]

        left = [blocks_of(part) for part in (0, 1 - core)]
        squares = [value.astype(jnp.float32) for value in left]
        squares = squares[0] * squares[0] + jnp.where(core == 0, squares[1] * squares[1], 0.0)
        norm = squares[:, :128]
        for slot in range(1, slots):
            norm = norm + squares[:, 128 * slot : 128 * (slot + 1)]
        lane = lax.broadcasted_iota(jnp.int32, (count, 8, 128), 2) // 32
        same = lax.broadcasted_iota(jnp.int32, (count, 16, 128), 1) // 4 == (
            lax.broadcasted_iota(jnp.int32, (count, 16, 128), 2) // 32
        )

        def queries_of(value):
            value = value[:, :8] + value[:, 8:]
            return value + pltpu.roll(value, 4, 1)

        low = jnp.zeros((count, 8, 128), jnp.float32)
        high = low
        for i in range(PARTS):
            right = jnp.concatenate(
                [
                    jnp.concatenate(
                        [train_part[i, slot, :, 128 * sub : 128 * (sub + 1)] for slot in range(slots)], axis=1
                    )
                    for sub in range(4)
                ],
                axis=0,
            )
            product = lax.dot_general(
                left[i % 2], right, (((1,), (1,)), ((), ())), preferred_element_type=jnp.float32
            ).reshape(count, 16, 128)
            value = queries_of(jnp.where(same, product, 0.0))
            value = value + pltpu.roll(value, 64, 2)
            value = value + pltpu.roll(value, 32, 2)
            low = low + jnp.where(lane == jnp.where(core == 0, i // 2, i), value, 0.0)
            if i >= 4:
                high = high + jnp.where(lane == i - 4, value, 0.0)
        norm = queries_of(norm.reshape(count, 16, 128))
        norm = jnp.broadcast_to(jnp.sum(norm, axis=2, keepdims=True), (count, 8, 128))
        for k, value in enumerate((low, high, norm)):
            for place, lev in enumerate(levels):
                scored[k, whos, pl.ds(lev, 1)] = value[many * place : many * (place + 1)].reshape(many, 1, 8, 128)

    def own_to_column(who):
        return remote(
            blocks_ref.at[pl.ds(2 * columns[who], 2)],
            gathered.at[:, who, level],
            q_send.at[who],
            q_recv.at[who],
            at(columns[who], level),
        )

    def block_of(lot, by):
        return gathered.at[:, LOTS[lot], shifted(by)]

    def near_copy(i, lot, source=0):
        block = block_of(lot, source)
        return remote(block, block, near_send.at[i, lot], near_recv.at[i, lot], at(column, shifted(NEAR[i])))

    def far_copy(row, lot, source, on):
        block = block_of(lot, source)
        return remote(block, block, far_send.at[row, lot], far_recv.at[row, lot], at(column, shifted(on)))

    far = [(row, lot, (-2, 2)[row], (1, -1)[row]) for lot in range(3) for row in range(2)]
    far += [(0, 3, -2, 2), (1, 4, 2, -2)]

    def own_to_level(i):
        to = shifted(-i)
        return remote(
            blocks_ref.at[to], gathered.at[0, OWN, level], q_send.at[i], q_recv.at[i], at(column, to)
        )

    def levels_to_column(who):
        return remote(
            gathered.at[0, OWN],
            gathered.at[0, who],
            across_send.at[who],
            across_recv.at[who],
            at(columns[who], level),
        )

    order = (4, 3, 5, 2, 6, 1, 7)

    @pl.when(core == 0)
    def _():
        for who in (FIRST, SECOND, ACROSS):
            own_to_column(who).start()
        for half in range(2):
            gathered[half, OWN, level] = blocks_ref[2 * column + half]
        for i in range(len(NEAR)):
            near_copy(i, 0).start()
        for half in range(2):
            train_to_column(ACROSS, half).start()
        for who in (FIRST, SECOND):
            train_to_column(who, 0).start()
        for who in (FIRST, SECOND):
            train_to_column(who, 1).start()
        for who in (FIRST, SECOND):
            own_to_column(who).wait_recv()
        for i in range(len(NEAR)):
            near_copy(i, 1).start()
        own_to_column(ACROSS).wait_recv()
        for i in range(len(NEAR)):
            near_copy(i, 2).start()
        for lot in range(3):
            for i in range(2):
                near_copy(i, lot, -NEAR[i]).wait_recv()
            for row, which, source, on in far:
                if which == lot or lot == 2 and which > 2:
                    far_copy(row, which, source, on).start()
        for lot in range(3):
            for i in range(2, len(NEAR)):
                near_copy(i, lot, -NEAR[i]).wait_recv()
        for half in range(2):
            keep_for_column(half).wait()
            for who in (FIRST, SECOND, ACROSS):
                train_to_column(who, half).wait_recv()
        score(slice(0, COLUMNS), [level] + [shifted(by) for by in NEAR])
        for row, lot, source, on in far:
            far_copy(row, lot, source - on, on).wait_recv()
        score(slice(0, COLUMNS), [shifted(by) for by in (3, 4, 5)])

    @pl.when(core == 1)
    def _():
        for i in order:
            own_to_level(i).start()
        for i in (2, 6, 1, 7, 3, 5, 4):
            train_to_level(i).start()
        gathered[0, OWN, level] = blocks_ref[level]
        for i in order:
            remote(
                blocks_ref.at[0],
                gathered.at[0, OWN, shifted(i)],
                q_send.at[i],
                q_recv.at[i],
                at(column, shifted(-i)),
            ).wait_recv()
        for who in (FIRST, SECOND, ACROSS):
            levels_to_column(who).start()
        keep_for_level().wait()
        for i in range(1, ring):
            train_to_level(i).wait_recv()
        score(slice(0, 1), list(range(ring)))
        for who in (ACROSS, FIRST, SECOND):
            levels_to_column(who).wait_recv()
        score(slice(1, COLUMNS), list(range(ring)))

    row = lax.broadcasted_iota(jnp.int32, (ring // 2, 8, 128), 1)
    per_column = tile_count // COLUMNS
    for who in range(COLUMNS):
        place = pl.ds(columns[who] * per_column, per_column)
        for k in range(3):
            value = scored[k, who].reshape(ring // 2, 2, 8, 128)
            tiles[place, :, 128 * k : 128 * (k + 1)] = jnp.where(row < 4, value[:, 0], value[:, 1])

    per_group = tile_count // groups

    def group_copy(d):
        to = lax.rem(group + d, groups)
        return remote(
            tiles.at[pl.ds(to * per_group, per_group)], tiles_in.at[d], r_send.at[d], r_recv.at[d], shard, to
        )

    for d in sorted(range(1, groups), key=lambda d: abs(2 * d - groups)):
        group_copy(d).start()
    sums = [tiles[pl.ds(group * per_group, per_group)], None]
    for d in range(1, groups):
        group_copy(d).wait_recv()
        sums[d % 2] = tiles_in[d] if sums[d % 2] is None else sums[d % 2] + tiles_in[d]
    by_column = jnp.where(core == 0, sums[0], sums[1])
    by_level = jnp.where(core == 0, sums[1], sums[0])

    scores_of = [by_column[:, :, :128]] * COLUMNS + [by_level[:, :, :128]] * 4 + [by_level[:, :, 128:256]] * 4
    squares_of = [by_column[:, :, 256:]] * COLUMNS + [by_level[:, :, 256:]] * ring
    is_score = lax.broadcasted_iota(jnp.int32, (per_group, 8, 128), 2) < 32

    def packed(j):
        turned = scores_of[j] if j % 4 == 0 else pltpu.roll(scores_of[j], 128 - 32 * (j % 4), 2)
        return jnp.where(is_score, turned, squares_of[j])

    def pair_copy(j):
        to = at(columns[j], level) if j < COLUMNS else at(column, shifted(j - COLUMNS))
        return remote(pair_out.at[j], pair_in.at[j], p_send.at[j], p_recv.at[j], to)

    others = [COLUMNS + i for i in (4, 3, 5)] + [ACROSS] + [COLUMNS + i for i in (2, 6)] + [FIRST, SECOND]
    others += [COLUMNS + i for i in (1, 7)]
    for j in others:
        pair_out[j] = packed(j)
        pair_copy(j).start()
    answer = packed(OWN) + packed(COLUMNS)
    for j in reversed(others):
        pair_copy(j).wait_recv()
        answer = answer + pair_in[j]
    out_ref[...] = (answer[:, :, :32] / jnp.sqrt(answer[:, :, 32:33] + EPSILON)).reshape(out_ref.shape)

    @pl.when(core == 0)
    def _():
        for half in range(2):
            for who in (FIRST, SECOND, ACROSS):
                train_to_column(who, half).wait_send()
        for who in (FIRST, SECOND, ACROSS):
            own_to_column(who).wait_send()
        for lot in range(3):
            for i in range(len(NEAR)):
                near_copy(i, lot).wait_send()
        for row, lot, source, on in far:
            far_copy(row, lot, source, on).wait_send()

    @pl.when(core == 1)
    def _():
        for i in range(1, ring):
            train_to_level(i).wait_send()
            own_to_level(i).wait_send()
        for who in (ACROSS, FIRST, SECOND):
            levels_to_column(who).wait_send()

    def tile_sent(d, carry):
        group_copy(d).wait_send()
        return carry

    lax.fori_loop(1, groups, tile_sent, 0)
    for j in others:
        pair_copy(j).wait_send()


def solution(mesh):
    shards, groups = mesh.shape["shard"], mesh.shape["layer"]
    ring = shards // COLUMNS

    def on_device(query_grads, out_basis, in_basis, eigen_scale, layer_slot, train_grads):
        local, slots, width = query_grads.shape
        side = out_basis.shape[1]
        rows = train_grads.shape[0]
        tile_count = local * shards // 8
        per_group = tile_count // groups
        dma = pltpu.SemaphoreType.DMA
        return pl.pallas_call(
            functools.partial(kernel, ring, groups),
            out_shape=jax.ShapeDtypeStruct((8 * per_group, rows), jnp.float32),
            in_specs=[pl.BlockSpec(memory_space=pl.ANY)] * 6,
            out_specs=pl.BlockSpec(memory_space=pltpu.VMEM),
            scratch_shapes=[
                pltpu.SMEM((slots,), jnp.int32),
                pltpu.VMEM((slots, local, width), jnp.bfloat16),
                pltpu.VMEM((slots, side, side), jnp.float32),
                pltpu.VMEM((slots, side, side), jnp.float32),
                pltpu.VMEM((slots, side, side), jnp.float32),
                pltpu.VMEM((slots, local * width // 128, 128), jnp.float32),
                pltpu.VMEM((slots, local * width // 128, 128), jnp.float32),
                pltpu.VMEM((PARTS, 16, 128 * slots), jnp.bfloat16),
                pltpu.VMEM((PARTS, slots, rows, width // PARTS), jnp.bfloat16),
                pltpu.VMEM((2, COLUMNS, ring, 16, 128 * slots), jnp.bfloat16),
                pltpu.VMEM((3, COLUMNS, ring, 8, 128), jnp.float32),
                pltpu.VMEM((tile_count, 8, 384), jnp.float32),
                pltpu.VMEM((groups, per_group, 8, 384), jnp.float32),
                pltpu.VMEM((COLUMNS + ring, per_group, 8, 128), jnp.float32),
                pltpu.VMEM((COLUMNS + ring, per_group, 8, 128), jnp.float32),
                dma((7,)),
                dma((PARTS,)),
                dma((PARTS,)),
                dma((ring,)),
                dma((ring,)),
                dma((len(NEAR), 3)),
                dma((len(NEAR), 3)),
                dma((2, 5)),
                dma((2, 5)),
                dma((COLUMNS,)),
                dma((COLUMNS,)),
                dma((groups,)),
                dma((groups,)),
                dma((COLUMNS + ring,)),
                dma((COLUMNS + ring,)),
            ],
            compiler_params=pltpu.CompilerParams(
                collective_id=0, has_side_effects=True, vmem_limit_bytes=VMEM_BYTES
            ),
        )(
            *[
                pltpu.with_memory_space_constraint(x, pltpu.HBM)
                for x in (
                    layer_slot,
                    jnp.transpose(query_grads, (1, 0, 2)),
                    out_basis,
                    in_basis,
                    eigen_scale,
                    jnp.transpose(train_grads, (1, 0, 2)),
                )
            ]
        )

    return jax.shard_map(
        on_device,
        mesh=mesh,
        in_specs=(
            P("shard", "layer", None),
            P("layer", None, None),
            P("layer", None, None),
            P("layer", None, None),
            P("layer"),
            P("shard", "layer", None),
        ),
        out_specs=P("layer", "shard"),
        check_vma=False,
    )
```

```python
import functools

import jax
import jax.numpy as jnp
from jax import lax
from jax.experimental import pallas as pl
from jax.experimental.pallas import tpu as pltpu
from jax.sharding import PartitionSpec as P

DAMPING = 0.05
EPSILON = 1e-06
MESH = pl.DeviceIdType.MESH
PARTS = 8
COLUMNS = 4
OWN, FIRST, SECOND, ACROSS = range(4)
NEAR = (2, -2, 1, -1)
LOTS = (slice(0, 1), slice(1, 3), slice(3, 4), slice(0, 2), slice(2, 4))
VMEM_BYTES = 40 * 1024 * 1024


def split(value):
    top = value.astype(jnp.bfloat16)
    return top, (value - top.astype(jnp.float32)).astype(jnp.bfloat16)


def product(left, right, contract):
    dims = (contract, ((), ()))
    total = None
    for i, a in enumerate(left):
        for b in right[: len(right) - i]:
            term = lax.dot_general(a, b, dims, preferred_element_type=jnp.float32)
            total = term if total is None else total + term
    return total


def precondition_slot(index, slot, q_ref, s_ref, a_ref, e_ref, rows_ref, turned_ref, blocks_ref):
    side = s_ref.shape[1]
    width = q_ref.shape[2]
    pieces = width // 128
    half = side // 2
    queries = q_ref[index].astype(jnp.float32)
    for piece in range(pieces):
        rows_ref[slot, 4 * piece : 4 * piece + 4, :] = queries[:, 128 * piece : 128 * (piece + 1)]
    basis = jnp.concatenate([s_ref[index, pl.ds(parity, half, stride=2), :] for parity in range(2)], axis=0)
    right = split(a_ref[index])
    scale = e_ref[index] + DAMPING
    stacked = []
    for n in range(4):
        both = rows_ref[slot, pl.ds(n, half, stride=4), :]
        stacked.append(jnp.concatenate([both[:, :side], both[:, side:]], axis=0))
    stacked = jnp.concatenate(stacked, axis=0)
    stacked = product((stacked.astype(jnp.bfloat16),), right, ((1,), (0,)))
    wide = jnp.concatenate([stacked[side * n : side * (n + 1)] for n in range(4)], axis=1)
    wide = product(split(basis.T), split(wide), ((1,), (0,)))
    wide = wide / jnp.concatenate([scale] * 4, axis=1)
    wide = product(split(basis), split(wide), ((1,), (0,)))
    stacked = jnp.concatenate([wide[:, side * n : side * (n + 1)] for n in range(4)], axis=0)
    stacked = product(split(stacked), right, ((1,), (1,)))
    for n in range(4):
        block = stacked[side * n : side * (n + 1)]
        turned_ref[slot, pl.ds(n, half, stride=4), :] = jnp.concatenate([block[:half], block[half:]], axis=1)
    for part in range(PARTS):
        blocks_ref[part, :, 128 * slot : 128 * (slot + 1)] = turned_ref[slot, 16 * part : 16 * (part + 1), :].astype(
            jnp.bfloat16
        )


def kernel(
    ring,
    groups,
    slot_hbm,
    q_hbm,
    s_hbm,
    a_hbm,
    e_hbm,
    train_ref,
    out_ref,
    slot_ref,
    q_ref,
    s_ref,
    a_ref,
    e_ref,
    rows_ref,
    turned_ref,
    blocks_ref,
    train_part,
    gathered,
    scored,
    tiles,
    tiles_in,
    summed,
    pair_out,
    pair_in,
    local_sem,
    t_send,
    t_recv,
    q_send,
    q_recv,
    near_send,
    near_recv,
    far_send,
    far_recv,
    across_send,
    across_recv,
    r_send,
    r_recv,
    p_send,
    p_recv,
):
    shard = lax.axis_index("shard")
    group = lax.axis_index("layer")
    core = lax.rem(group, 2)
    column = shard // ring
    level = lax.rem(shard, ring)
    slots = q_ref.shape[0]
    tile_count = tiles.shape[0]

    def at(col, lev):
        return col * ring + lev

    def shifted(by):
        return lax.rem(level + by + ring, ring)

    first = column + 1 - 2 * lax.rem(column, 2)
    second = 3 - column
    across = 3 - first
    columns = [column, first, second, across]

    def remote(src, dst, send, recv, to_shard, to_group=group):
        return pltpu.make_async_remote_copy(
            src_ref=src, dst_ref=dst, send_sem=send, recv_sem=recv, device_id=(to_shard, to_group), device_id_type=MESH
        )

    loads = []
    for i, (src, dst) in enumerate(
        [(q_hbm, q_ref), (a_hbm, a_ref), (s_hbm, s_ref), (e_hbm, e_ref), (slot_hbm, slot_ref)]
    ):
        copy = pltpu.make_async_copy(src, dst, local_sem.at[i])
        copy.start()
        loads.append(copy)


    barrier = pltpu.get_barrier_semaphore()
    partners = [(at(column, shifted(by)), group) for by in range(1, ring)]
    partners += [(at(c, level), group) for c in columns[1:]]
    for who in partners:
        pl.semaphore_signal(barrier, inc=1, device_id=who, device_id_type=MESH)

    def greet(d, carry):
        pl.semaphore_signal(barrier, inc=1, device_id=(shard, lax.rem(group + d, groups)), device_id_type=MESH)
        return carry

    lax.fori_loop(1, groups, greet, 0)
    span = train_ref.shape[2] // PARTS

    def part_of_train(part):
        return train_ref.at[:, :, pl.ds(pl.multiple_of(part * span, 128), span)]

    def train_to_column(who, half):
        i = 2 * who + half
        return remote(
            part_of_train(2 * columns[who] + half), train_part.at[i], t_send.at[i], t_recv.at[i], at(columns[who], level)
        )

    def train_to_level(i):
        to = shifted(-i)
        return remote(part_of_train(to), train_part.at[i], t_send.at[i], t_recv.at[i], at(column, to))

    def keep_for_column(half):
        return pltpu.make_async_copy(
            part_of_train(2 * column + half), train_part.at[half], local_sem.at[len(loads) + half]
        )

    def keep_for_level():
        return pltpu.make_async_copy(part_of_train(level), train_part.at[0], local_sem.at[len(loads)])

    @pl.when(core == 0)
    def _():
        for half in range(2):
            keep_for_column(half).start()

    @pl.when(core == 1)
    def _():
        keep_for_level().start()

    for copy in loads:
        copy.wait()
    for slot in range(slots):
        index = lax.rem(slot_ref[slot], slots)
        precondition_slot(index, slot, q_ref, s_ref, a_ref, e_ref, rows_ref, turned_ref, blocks_ref)

    pl.semaphore_wait(barrier, len(partners) + groups - 1)

    def score(whos, levels):
        many = whos.stop - whos.start
        count = many * len(levels)

        def blocks_of(part):
            value = [gathered[part, whos, pl.ds(lev, 1)].reshape(16 * many, 128 * slots) for lev in levels]
            return jnp.concatenate(value, axis=0) if len(value) > 1 else value[0]

        left = [blocks_of(part) for part in (0, 1 - core)]
        squares = [value.astype(jnp.float32) for value in left]
        squares = squares[0] * squares[0] + jnp.where(core == 0, squares[1] * squares[1], 0.0)
        norm = squares[:, :128]
        for slot in range(1, slots):
            norm = norm + squares[:, 128 * slot : 128 * (slot + 1)]
        lane = lax.broadcasted_iota(jnp.int32, (count, 8, 128), 2) // 32
        same = lax.broadcasted_iota(jnp.int32, (count, 16, 128), 1) // 4 == (
            lax.broadcasted_iota(jnp.int32, (count, 16, 128), 2) // 32
        )

        def queries_of(value):
            value = value[:, :8] + value[:, 8:]
            return value + pltpu.roll(value, 4, 1)

        low = jnp.zeros((count, 8, 128), jnp.float32)
        high = low
        for i in range(PARTS):
            right = jnp.concatenate(
                [
                    jnp.concatenate(
                        [train_part[i, slot, :, 128 * sub : 128 * (sub + 1)] for slot in range(slots)], axis=1
                    )
                    for sub in range(4)
                ],
                axis=0,
            )
            product = lax.dot_general(
                left[i % 2], right, (((1,), (1,)), ((), ())), preferred_element_type=jnp.float32
            ).reshape(count, 16, 128)
            value = queries_of(jnp.where(same, product, 0.0))
            value = value + pltpu.roll(value, 64, 2)
            value = value + pltpu.roll(value, 32, 2)
            low = low + jnp.where(lane == jnp.where(core == 0, i // 2, i), value, 0.0)
            if i >= 4:
                high = high + jnp.where(lane == i - 4, value, 0.0)
        norm = queries_of(norm.reshape(count, 16, 128))
        norm = jnp.broadcast_to(jnp.sum(norm, axis=2, keepdims=True), (count, 8, 128))
        for k, value in enumerate((low, high, norm)):
            for place, lev in enumerate(levels):
                scored[k, whos, pl.ds(lev, 1)] = value[many * place : many * (place + 1)].reshape(many, 1, 8, 128)

    def own_to_column(who):
        return remote(
            blocks_ref.at[pl.ds(2 * columns[who], 2)],
            gathered.at[:, who, level],
            q_send.at[who],
            q_recv.at[who],
            at(columns[who], level),
        )

    def block_of(lot, by):
        return gathered.at[:, LOTS[lot], shifted(by)]

    def near_copy(i, lot, source=0):
        block = block_of(lot, source)
        return remote(block, block, near_send.at[i, lot], near_recv.at[i, lot], at(column, shifted(NEAR[i])))

    def far_copy(row, lot, source, on):
        block = block_of(lot, source)
        return remote(block, block, far_send.at[row, lot], far_recv.at[row, lot], at(column, shifted(on)))

    far = [(row, lot, (-2, 2)[row], (1, -1)[row]) for lot in range(3) for row in range(2)]
    far += [(0, 3, -2, 2), (1, 4, 2, -2)]

    def own_to_level(i):
        to = shifted(-i)
        return remote(
            blocks_ref.at[to], gathered.at[0, OWN, level], q_send.at[i], q_recv.at[i], at(column, to)
        )

    def levels_to_column(who):
        return remote(
            gathered.at[0, OWN],
            gathered.at[0, who],
            across_send.at[who],
            across_recv.at[who],
            at(columns[who], level),
        )

    order = (4, 3, 5, 2, 6, 1, 7)

    @pl.when(core == 0)
    def _():
        for who in (FIRST, SECOND, ACROSS):
            own_to_column(who).start()
        for half in range(2):
            gathered[half, OWN, level] = blocks_ref[2 * column + half]
        for i in range(len(NEAR)):
            near_copy(i, 0).start()
        for half in range(2):
            train_to_column(ACROSS, half).start()
        for who in (FIRST, SECOND):
            train_to_column(who, 0).start()
        for who in (FIRST, SECOND):
            train_to_column(who, 1).start()
        for who in (FIRST, SECOND):
            own_to_column(who).wait_recv()
        for i in range(len(NEAR)):
            near_copy(i, 1).start()
        own_to_column(ACROSS).wait_recv()
        for i in range(len(NEAR)):
            near_copy(i, 2).start()
        for lot in range(3):
            for i in range(2):
                near_copy(i, lot, -NEAR[i]).wait_recv()
            for row, which, source, on in far:
                if which == lot or lot == 2 and which > 2:
                    far_copy(row, which, source, on).start()
        for lot in range(3):
            for i in range(2, len(NEAR)):
                near_copy(i, lot, -NEAR[i]).wait_recv()
        for half in range(2):
            keep_for_column(half).wait()
            for who in (FIRST, SECOND, ACROSS):
                train_to_column(who, half).wait_recv()
        score(slice(0, COLUMNS), [level] + [shifted(by) for by in NEAR])
        for row, lot, source, on in far:
            far_copy(row, lot, source - on, on).wait_recv()
        score(slice(0, COLUMNS), [shifted(by) for by in (3, 4, 5)])

    @pl.when(core == 1)
    def _():
        for i in order:
            own_to_level(i).start()
        for i in (2, 6, 1, 7, 3, 5, 4):
            train_to_level(i).start()
        gathered[0, OWN, level] = blocks_ref[level]
        for i in order:
            remote(
                blocks_ref.at[0],
                gathered.at[0, OWN, shifted(i)],
                q_send.at[i],
                q_recv.at[i],
                at(column, shifted(-i)),
            ).wait_recv()
        for who in (FIRST, SECOND, ACROSS):
            levels_to_column(who).start()
        keep_for_level().wait()
        for i in range(1, ring):
            train_to_level(i).wait_recv()
        score(slice(0, 1), list(range(ring)))
        for who in (ACROSS, FIRST, SECOND):
            levels_to_column(who).wait_recv()
        score(slice(1, COLUMNS), list(range(ring)))

    row = lax.broadcasted_iota(jnp.int32, (ring // 2, 8, 128), 1)
    per_column = tile_count // COLUMNS
    for who in range(COLUMNS):
        place = pl.ds(columns[who] * per_column, per_column)
        for k in range(3):
            value = scored[k, who].reshape(ring // 2, 2, 8, 128)
            tiles[place, :, 128 * k : 128 * (k + 1)] = jnp.where(row < 4, value[:, 0], value[:, 1])

    per_group = tile_count // groups

    def group_copy(d):
        to = lax.rem(group + d, groups)
        return remote(
            tiles.at[pl.ds(to * per_group, per_group)], tiles_in.at[d], r_send.at[d], r_recv.at[d], shard, to
        )

    for d in sorted(range(1, groups), key=lambda d: abs(2 * d - groups)):
        group_copy(d).start()

    def sum_of(which):
        def add(even):
            value = tiles[pl.ds(group * per_group, per_group)] if even else None
            for d in range(2 if even else 1, groups, 2):
                group_copy(d).wait_recv()
                value = tiles_in[d] if value is None else value + tiles_in[d]
            summed[which] = value

        @pl.when(core == which)
        def _():
            add(True)

        @pl.when(core != which)
        def _():
            add(False)

    is_score = lax.broadcasted_iota(jnp.int32, (per_group, 8, 128), 2) < 32

    def packed(j):
        which = 0 if j < COLUMNS else 1
        start = 128 if j >= COLUMNS + 4 else 0
        scores = summed[which, :, :, start : start + 128]
        turned = scores if j % 4 == 0 else pltpu.roll(scores, 128 - 32 * (j % 4), 2)
        return jnp.where(is_score, turned, summed[which, :, :, 256:])

    def pair_copy(j):
        to = at(columns[j], level) if j < COLUMNS else at(column, shifted(j - COLUMNS))
        return remote(pair_out.at[j], pair_in.at[j], p_send.at[j], p_recv.at[j], to)

    from_levels = [COLUMNS + i for i in (4, 3, 5, 2, 6, 1, 7)]
    from_columns = [ACROSS, FIRST, SECOND]
    others = from_levels + from_columns
    sum_of(1)
    for j in from_levels:
        pair_out[j] = packed(j)
        pair_copy(j).start()
    sum_of(0)
    for j in from_columns:
        pair_out[j] = packed(j)
        pair_copy(j).start()
    answer = packed(OWN) + packed(COLUMNS)
    for j in reversed(from_levels):
        pair_copy(j).wait_recv()
        answer = answer + pair_in[j]
    for j in reversed(from_columns):
        pair_copy(j).wait_recv()
        answer = answer + pair_in[j]
    out_ref[...] = (answer[:, :, :32] / jnp.sqrt(answer[:, :, 32:33] + EPSILON)).reshape(out_ref.shape)

    @pl.when(core == 0)
    def _():
        for half in range(2):
            for who in (FIRST, SECOND, ACROSS):
                train_to_column(who, half).wait_send()
        for who in (FIRST, SECOND, ACROSS):
            own_to_column(who).wait_send()
        for lot in range(3):
            for i in range(len(NEAR)):
                near_copy(i, lot).wait_send()
        for row, lot, source, on in far:
            far_copy(row, lot, source, on).wait_send()

    @pl.when(core == 1)
    def _():
        for i in range(1, ring):
            train_to_level(i).wait_send()
            own_to_level(i).wait_send()
        for who in (ACROSS, FIRST, SECOND):
            levels_to_column(who).wait_send()

    def tile_sent(d, carry):
        group_copy(d).wait_send()
        return carry

    lax.fori_loop(1, groups, tile_sent, 0)
    for j in others:
        pair_copy(j).wait_send()


def solution(mesh):
    shards, groups = mesh.shape["shard"], mesh.shape["layer"]
    ring = shards // COLUMNS

    def on_device(query_grads, out_basis, in_basis, eigen_scale, layer_slot, train_grads):
        local, slots, width = query_grads.shape
        side = out_basis.shape[1]
        rows = train_grads.shape[0]
        tile_count = local * shards // 8
        per_group = tile_count // groups
        dma = pltpu.SemaphoreType.DMA
        return pl.pallas_call(
            functools.partial(kernel, ring, groups),
            out_shape=jax.ShapeDtypeStruct((8 * per_group, rows), jnp.float32),
            in_specs=[pl.BlockSpec(memory_space=pl.ANY)] * 6,
            out_specs=pl.BlockSpec(memory_space=pltpu.VMEM),
            scratch_shapes=[
                pltpu.SMEM((slots,), jnp.int32),
                pltpu.VMEM((slots, local, width), jnp.bfloat16),
                pltpu.VMEM((slots, side, side), jnp.float32),
                pltpu.VMEM((slots, side, side), jnp.float32),
                pltpu.VMEM((slots, side, side), jnp.float32),
                pltpu.VMEM((slots, local * width // 128, 128), jnp.float32),
                pltpu.VMEM((slots, local * width // 128, 128), jnp.float32),
                pltpu.VMEM((PARTS, 16, 128 * slots), jnp.bfloat16),
                pltpu.VMEM((PARTS, slots, rows, width // PARTS), jnp.bfloat16),
                pltpu.VMEM((2, COLUMNS, ring, 16, 128 * slots), jnp.bfloat16),
                pltpu.VMEM((3, COLUMNS, ring, 8, 128), jnp.float32),
                pltpu.VMEM((tile_count, 8, 384), jnp.float32),
                pltpu.VMEM((groups, per_group, 8, 384), jnp.float32),
                pltpu.VMEM((2, per_group, 8, 384), jnp.float32),
                pltpu.VMEM((COLUMNS + ring, per_group, 8, 128), jnp.float32),
                pltpu.VMEM((COLUMNS + ring, per_group, 8, 128), jnp.float32),
                dma((7,)),
                dma((PARTS,)),
                dma((PARTS,)),
                dma((ring,)),
                dma((ring,)),
                dma((len(NEAR), 3)),
                dma((len(NEAR), 3)),
                dma((2, 5)),
                dma((2, 5)),
                dma((COLUMNS,)),
                dma((COLUMNS,)),
                dma((groups,)),
                dma((groups,)),
                dma((COLUMNS + ring,)),
                dma((COLUMNS + ring,)),
            ],
            compiler_params=pltpu.CompilerParams(
                collective_id=0, has_side_effects=True, vmem_limit_bytes=VMEM_BYTES
            ),
        )(
            *[
                pltpu.with_memory_space_constraint(x, pltpu.HBM)
                for x in (
                    layer_slot,
                    jnp.transpose(query_grads, (1, 0, 2)),
                    out_basis,
                    in_basis,
                    eigen_scale,
                    jnp.transpose(train_grads, (1, 0, 2)),
                )
            ]
        )

    return jax.shard_map(
        on_device,
        mesh=mesh,
        in_specs=(
            P("shard", "layer", None),
            P("layer", None, None),
            P("layer", None, None),
            P("layer", None, None),
            P("layer"),
            P("shard", "layer", None),
        ),
        out_specs=P("layer", "shard"),
        check_vma=False,
    )
```

```python
import functools

import jax
import jax.numpy as jnp
from jax import lax
from jax.experimental import pallas as pl
from jax.experimental.pallas import tpu as pltpu
from jax.sharding import PartitionSpec as P

DAMPING = 0.05
EPSILON = 1e-06
MESH = pl.DeviceIdType.MESH
PARTS = 8
COLUMNS = 4
OWN, FIRST, SECOND, ACROSS = range(4)
NEAR = (2, -2, 1, -1)
LOTS = (slice(0, 1), slice(1, 3), slice(3, 4), slice(0, 2), slice(2, 4))
VMEM_BYTES = 40 * 1024 * 1024


def split(value):
    top = value.astype(jnp.bfloat16)
    return top, (value - top.astype(jnp.float32)).astype(jnp.bfloat16)


def product(left, right, contract):
    dims = (contract, ((), ()))
    total = None
    for i, a in enumerate(left):
        for b in right[: len(right) - i]:
            term = lax.dot_general(a, b, dims, preferred_element_type=jnp.float32)
            total = term if total is None else total + term
    return total


def precondition_slot(index, slot, q_ref, s_ref, a_ref, e_ref, rows_ref, turned_ref, blocks_ref):
    side = s_ref.shape[1]
    width = q_ref.shape[2]
    pieces = width // 128
    half = side // 2
    queries = q_ref[index].astype(jnp.float32)
    for piece in range(pieces):
        rows_ref[slot, 4 * piece : 4 * piece + 4, :] = queries[:, 128 * piece : 128 * (piece + 1)]
    basis = jnp.concatenate([s_ref[index, pl.ds(parity, half, stride=2), :] for parity in range(2)], axis=0)
    right = split(a_ref[index])
    scale = e_ref[index] + DAMPING
    stacked = []
    for n in range(4):
        both = rows_ref[slot, pl.ds(n, half, stride=4), :]
        stacked.append(jnp.concatenate([both[:, :side], both[:, side:]], axis=0))
    stacked = jnp.concatenate(stacked, axis=0)
    stacked = product((stacked.astype(jnp.bfloat16),), right, ((1,), (0,)))
    wide = jnp.concatenate([stacked[side * n : side * (n + 1)] for n in range(4)], axis=1)
    wide = product(split(basis.T), split(wide), ((1,), (0,)))
    wide = wide / jnp.concatenate([scale] * 4, axis=1)
    wide = product(split(basis), split(wide), ((1,), (0,)))
    stacked = jnp.concatenate([wide[:, side * n : side * (n + 1)] for n in range(4)], axis=0)
    stacked = product(split(stacked), right, ((1,), (1,)))
    for n in range(4):
        block = stacked[side * n : side * (n + 1)]
        turned_ref[slot, pl.ds(n, half, stride=4), :] = jnp.concatenate([block[:half], block[half:]], axis=1)
    for part in range(PARTS):
        blocks_ref[part, :, 128 * slot : 128 * (slot + 1)] = turned_ref[slot, 16 * part : 16 * (part + 1), :].astype(
            jnp.bfloat16
        )


def kernel(
    ring,
    groups,
    slot_hbm,
    q_hbm,
    s_hbm,
    a_hbm,
    e_hbm,
    train_ref,
    out_ref,
    slot_ref,
    q_ref,
    s_ref,
    a_ref,
    e_ref,
    rows_ref,
    turned_ref,
    blocks_ref,
    train_part,
    gathered,
    scored,
    tiles,
    tiles_in,
    summed,
    pair_out,
    pair_in,
    local_sem,
    t_send,
    t_recv,
    q_send,
    q_recv,
    near_send,
    near_recv,
    far_send,
    far_recv,
    across_send,
    across_recv,
    r_send,
    r_recv,
    p_send,
    p_recv,
):
    shard = lax.axis_index("shard")
    group = lax.axis_index("layer")
    core = lax.rem(group, 2)
    column = shard // ring
    level = lax.rem(shard, ring)
    slots = q_ref.shape[0]
    tile_count = tiles.shape[0]

    def at(col, lev):
        return col * ring + lev

    def shifted(by):
        return lax.rem(level + by + ring, ring)

    first = column + 1 - 2 * lax.rem(column, 2)
    second = 3 - column
    across = 3 - first
    columns = [column, first, second, across]

    def remote(src, dst, send, recv, to_shard, to_group=group):
        return pltpu.make_async_remote_copy(
            src_ref=src, dst_ref=dst, send_sem=send, recv_sem=recv, device_id=(to_shard, to_group), device_id_type=MESH
        )

    loads = []
    for i, (src, dst) in enumerate(
        [(q_hbm, q_ref), (a_hbm, a_ref), (s_hbm, s_ref), (e_hbm, e_ref), (slot_hbm, slot_ref)]
    ):
        copy = pltpu.make_async_copy(src, dst, local_sem.at[i])
        copy.start()
        loads.append(copy)


    barrier = pltpu.get_barrier_semaphore()
    partners = [(at(column, shifted(by)), group) for by in range(1, ring)]
    partners += [(at(c, level), group) for c in columns[1:]]
    for who in partners:
        pl.semaphore_signal(barrier, inc=1, device_id=who, device_id_type=MESH)

    def greet(d, carry):
        pl.semaphore_signal(barrier, inc=1, device_id=(shard, lax.rem(group + d, groups)), device_id_type=MESH)
        return carry

    lax.fori_loop(1, groups, greet, 0)
    span = train_ref.shape[2] // PARTS

    def part_of_train(part):
        return train_ref.at[:, :, pl.ds(pl.multiple_of(part * span, 128), span)]

    def train_to_column(who, half):
        i = 2 * who + half
        return remote(
            part_of_train(2 * columns[who] + half), train_part.at[i], t_send.at[i], t_recv.at[i], at(columns[who], level)
        )

    def train_to_level(i):
        to = shifted(-i)
        return remote(part_of_train(to), train_part.at[i], t_send.at[i], t_recv.at[i], at(column, to))

    def keep_for_column(half):
        return pltpu.make_async_copy(
            part_of_train(2 * column + half), train_part.at[half], local_sem.at[len(loads) + half]
        )

    def keep_for_level():
        return pltpu.make_async_copy(part_of_train(level), train_part.at[0], local_sem.at[len(loads)])

    @pl.when(core == 0)
    def _():
        for half in range(2):
            keep_for_column(half).start()

    @pl.when(core == 1)
    def _():
        keep_for_level().start()

    for copy in loads:
        copy.wait()
    for slot in range(slots):
        index = lax.rem(slot_ref[slot], slots)
        precondition_slot(index, slot, q_ref, s_ref, a_ref, e_ref, rows_ref, turned_ref, blocks_ref)

    pl.semaphore_wait(barrier, len(partners) + groups - 1)

    def score(whos, levels):
        many = whos.stop - whos.start
        count = many * len(levels)

        def blocks_of(part):
            value = [gathered[part, whos, pl.ds(lev, 1)].reshape(16 * many, 128 * slots) for lev in levels]
            return jnp.concatenate(value, axis=0) if len(value) > 1 else value[0]

        left = [blocks_of(part) for part in (0, 1 - core)]
        squares = [value.astype(jnp.float32) for value in left]
        squares = squares[0] * squares[0] + jnp.where(core == 0, squares[1] * squares[1], 0.0)
        norm = squares[:, :128]
        for slot in range(1, slots):
            norm = norm + squares[:, 128 * slot : 128 * (slot + 1)]
        lane = lax.broadcasted_iota(jnp.int32, (count, 8, 128), 2) // 32
        same = lax.broadcasted_iota(jnp.int32, (count, 16, 128), 1) // 4 == (
            lax.broadcasted_iota(jnp.int32, (count, 16, 128), 2) // 32
        )

        def queries_of(value):
            value = value[:, :8] + value[:, 8:]
            return value + pltpu.roll(value, 4, 1)

        low = jnp.zeros((count, 8, 128), jnp.float32)
        high = low
        for i in range(PARTS):
            right = jnp.concatenate(
                [
                    jnp.concatenate(
                        [train_part[i, slot, :, 128 * sub : 128 * (sub + 1)] for slot in range(slots)], axis=1
                    )
                    for sub in range(4)
                ],
                axis=0,
            )
            product = lax.dot_general(
                left[i % 2], right, (((1,), (1,)), ((), ())), preferred_element_type=jnp.float32
            ).reshape(count, 16, 128)
            value = queries_of(jnp.where(same, product, 0.0))
            value = value + pltpu.roll(value, 64, 2)
            value = value + pltpu.roll(value, 32, 2)
            low = low + jnp.where(lane == jnp.where(core == 0, i // 2, i), value, 0.0)
            if i >= 4:
                high = high + jnp.where(lane == i - 4, value, 0.0)
        norm = queries_of(norm.reshape(count, 16, 128))
        norm = jnp.broadcast_to(jnp.sum(norm, axis=2, keepdims=True), (count, 8, 128))
        for k, value in enumerate((low, high, norm)):
            for place, lev in enumerate(levels):
                scored[k, whos, pl.ds(lev, 1)] = value[many * place : many * (place + 1)].reshape(many, 1, 8, 128)

    def own_to_column(who):
        return remote(
            blocks_ref.at[pl.ds(2 * columns[who], 2)],
            gathered.at[:, who, level],
            q_send.at[who],
            q_recv.at[who],
            at(columns[who], level),
        )

    def block_of(lot, by):
        return gathered.at[:, LOTS[lot], shifted(by)]

    def near_copy(i, lot, source=0):
        block = block_of(lot, source)
        return remote(block, block, near_send.at[i, lot], near_recv.at[i, lot], at(column, shifted(NEAR[i])))

    def far_copy(row, lot, source, on):
        block = block_of(lot, source)
        return remote(block, block, far_send.at[row, lot], far_recv.at[row, lot], at(column, shifted(on)))

    far = [(row, lot, (-2, 2)[row], (1, -1)[row]) for lot in range(3) for row in range(2)]
    far += [(0, 3, -2, 2), (1, 4, 2, -2)]

    def own_to_level(i):
        to = shifted(-i)
        return remote(
            blocks_ref.at[to], gathered.at[0, OWN, level], q_send.at[i], q_recv.at[i], at(column, to)
        )

    def levels_to_column(who):
        return remote(
            gathered.at[0, OWN],
            gathered.at[0, who],
            across_send.at[who],
            across_recv.at[who],
            at(columns[who], level),
        )

    order = (4, 3, 5, 2, 6, 1, 7)

    @pl.when(core == 0)
    def _():
        for who in (FIRST, SECOND, ACROSS):
            own_to_column(who).start()
        for half in range(2):
            gathered[half, OWN, level] = blocks_ref[2 * column + half]
        for i in range(len(NEAR)):
            near_copy(i, 0).start()
        for half in range(2):
            for who in (ACROSS, FIRST, SECOND):
                train_to_column(who, half).start()
        for who in (FIRST, SECOND):
            own_to_column(who).wait_recv()
        for i in range(len(NEAR)):
            near_copy(i, 1).start()
        own_to_column(ACROSS).wait_recv()
        for i in range(len(NEAR)):
            near_copy(i, 2).start()
        for lot in range(3):
            for i in range(2):
                near_copy(i, lot, -NEAR[i]).wait_recv()
            for row, which, source, on in far:
                if which == lot or lot == 2 and which > 2:
                    far_copy(row, which, source, on).start()
        for lot in range(3):
            for i in range(2, len(NEAR)):
                near_copy(i, lot, -NEAR[i]).wait_recv()
        for half in range(2):
            keep_for_column(half).wait()
            for who in (FIRST, SECOND, ACROSS):
                train_to_column(who, half).wait_recv()
        score(slice(0, COLUMNS), [level] + [shifted(by) for by in NEAR])
        for row, lot, source, on in far:
            far_copy(row, lot, source - on, on).wait_recv()
        score(slice(0, COLUMNS), [shifted(by) for by in (3, 4, 5)])

    @pl.when(core == 1)
    def _():
        for i in order:
            own_to_level(i).start()
        for i in (2, 6, 1, 7, 3, 5, 4):
            train_to_level(i).start()
        gathered[0, OWN, level] = blocks_ref[level]
        for i in order:
            remote(
                blocks_ref.at[0],
                gathered.at[0, OWN, shifted(i)],
                q_send.at[i],
                q_recv.at[i],
                at(column, shifted(-i)),
            ).wait_recv()
        for who in (FIRST, SECOND, ACROSS):
            levels_to_column(who).start()
        keep_for_level().wait()
        for i in range(1, ring):
            train_to_level(i).wait_recv()
        score(slice(0, 1), list(range(ring)))
        for who in (ACROSS, FIRST, SECOND):
            levels_to_column(who).wait_recv()
        score(slice(1, COLUMNS), list(range(ring)))

    row = lax.broadcasted_iota(jnp.int32, (ring // 2, 8, 128), 1)
    per_column = tile_count // COLUMNS
    for who in range(COLUMNS):
        place = pl.ds(columns[who] * per_column, per_column)
        for k in range(3):
            value = scored[k, who].reshape(ring // 2, 2, 8, 128)
            tiles[place, :, 128 * k : 128 * (k + 1)] = jnp.where(row < 4, value[:, 0], value[:, 1])

    per_group = tile_count // groups

    def group_copy(d):
        to = lax.rem(group + d, groups)
        return remote(
            tiles.at[pl.ds(to * per_group, per_group)], tiles_in.at[d], r_send.at[d], r_recv.at[d], shard, to
        )

    for d in sorted(range(1, groups), key=lambda d: abs(2 * d - groups)):
        group_copy(d).start()

    def sum_of(which):
        def add(even):
            value = tiles[pl.ds(group * per_group, per_group)] if even else None
            for d in range(2 if even else 1, groups, 2):
                group_copy(d).wait_recv()
                value = tiles_in[d] if value is None else value + tiles_in[d]
            summed[which] = value

        @pl.when(core == which)
        def _():
            add(True)

        @pl.when(core != which)
        def _():
            add(False)

    is_score = lax.broadcasted_iota(jnp.int32, (per_group, 8, 128), 2) < 32

    def packed(j):
        which = 0 if j < COLUMNS else 1
        start = 128 if j >= COLUMNS + 4 else 0
        scores = summed[which, :, :, start : start + 128]
        turned = scores if j % 4 == 0 else pltpu.roll(scores, 128 - 32 * (j % 4), 2)
        return jnp.where(is_score, turned, summed[which, :, :, 256:])

    def pair_copy(j):
        to = at(columns[j], level) if j < COLUMNS else at(column, shifted(j - COLUMNS))
        return remote(pair_out.at[j], pair_in.at[j], p_send.at[j], p_recv.at[j], to)

    from_levels = [COLUMNS + i for i in (4, 3, 5, 2, 6, 1, 7)]
    from_columns = [ACROSS, FIRST, SECOND]
    others = from_levels + from_columns
    sum_of(1)
    for j in from_levels:
        pair_out[j] = packed(j)
        pair_copy(j).start()
    sum_of(0)
    for j in from_columns:
        pair_out[j] = packed(j)
        pair_copy(j).start()
    answer = packed(OWN) + packed(COLUMNS)
    for j in reversed(from_levels):
        pair_copy(j).wait_recv()
        answer = answer + pair_in[j]
    for j in reversed(from_columns):
        pair_copy(j).wait_recv()
        answer = answer + pair_in[j]
    out_ref[...] = (answer[:, :, :32] / jnp.sqrt(answer[:, :, 32:33] + EPSILON)).reshape(out_ref.shape)

    @pl.when(core == 0)
    def _():
        for half in range(2):
            for who in (FIRST, SECOND, ACROSS):
                train_to_column(who, half).wait_send()
        for who in (FIRST, SECOND, ACROSS):
            own_to_column(who).wait_send()
        for lot in range(3):
            for i in range(len(NEAR)):
                near_copy(i, lot).wait_send()
        for row, lot, source, on in far:
            far_copy(row, lot, source, on).wait_send()

    @pl.when(core == 1)
    def _():
        for i in range(1, ring):
            train_to_level(i).wait_send()
            own_to_level(i).wait_send()
        for who in (ACROSS, FIRST, SECOND):
            levels_to_column(who).wait_send()

    def tile_sent(d, carry):
        group_copy(d).wait_send()
        return carry

    lax.fori_loop(1, groups, tile_sent, 0)
    for j in others:
        pair_copy(j).wait_send()


def solution(mesh):
    shards, groups = mesh.shape["shard"], mesh.shape["layer"]
    ring = shards // COLUMNS

    def on_device(query_grads, out_basis, in_basis, eigen_scale, layer_slot, train_grads):
        local, slots, width = query_grads.shape
        side = out_basis.shape[1]
        rows = train_grads.shape[0]
        tile_count = local * shards // 8
        per_group = tile_count // groups
        dma = pltpu.SemaphoreType.DMA
        return pl.pallas_call(
            functools.partial(kernel, ring, groups),
            out_shape=jax.ShapeDtypeStruct((8 * per_group, rows), jnp.float32),
            in_specs=[pl.BlockSpec(memory_space=pl.ANY)] * 6,
            out_specs=pl.BlockSpec(memory_space=pltpu.VMEM),
            scratch_shapes=[
                pltpu.SMEM((slots,), jnp.int32),
                pltpu.VMEM((slots, local, width), jnp.bfloat16),
                pltpu.VMEM((slots, side, side), jnp.float32),
                pltpu.VMEM((slots, side, side), jnp.float32),
                pltpu.VMEM((slots, side, side), jnp.float32),
                pltpu.VMEM((slots, local * width // 128, 128), jnp.float32),
                pltpu.VMEM((slots, local * width // 128, 128), jnp.float32),
                pltpu.VMEM((PARTS, 16, 128 * slots), jnp.bfloat16),
                pltpu.VMEM((PARTS, slots, rows, width // PARTS), jnp.bfloat16),
                pltpu.VMEM((2, COLUMNS, ring, 16, 128 * slots), jnp.bfloat16),
                pltpu.VMEM((3, COLUMNS, ring, 8, 128), jnp.float32),
                pltpu.VMEM((tile_count, 8, 384), jnp.float32),
                pltpu.VMEM((groups, per_group, 8, 384), jnp.float32),
                pltpu.VMEM((2, per_group, 8, 384), jnp.float32),
                pltpu.VMEM((COLUMNS + ring, per_group, 8, 128), jnp.float32),
                pltpu.VMEM((COLUMNS + ring, per_group, 8, 128), jnp.float32),
                dma((7,)),
                dma((PARTS,)),
                dma((PARTS,)),
                dma((ring,)),
                dma((ring,)),
                dma((len(NEAR), 3)),
                dma((len(NEAR), 3)),
                dma((2, 5)),
                dma((2, 5)),
                dma((COLUMNS,)),
                dma((COLUMNS,)),
                dma((groups,)),
                dma((groups,)),
                dma((COLUMNS + ring,)),
                dma((COLUMNS + ring,)),
            ],
            compiler_params=pltpu.CompilerParams(
                collective_id=0, has_side_effects=True, vmem_limit_bytes=VMEM_BYTES
            ),
        )(
            *[
                pltpu.with_memory_space_constraint(x, pltpu.HBM)
                for x in (
                    layer_slot,
                    jnp.transpose(query_grads, (1, 0, 2)),
                    out_basis,
                    in_basis,
                    eigen_scale,
                    jnp.transpose(train_grads, (1, 0, 2)),
                )
            ]
        )

    return jax.shard_map(
        on_device,
        mesh=mesh,
        in_specs=(
            P("shard", "layer", None),
            P("layer", None, None),
            P("layer", None, None),
            P("layer", None, None),
            P("layer"),
            P("shard", "layer", None),
        ),
        out_specs=P("layer", "shard"),
        check_vma=False,
    )
```

```python
import functools

import jax
import jax.numpy as jnp
from jax import lax
from jax.experimental import pallas as pl
from jax.experimental.pallas import tpu as pltpu
from jax.sharding import PartitionSpec as P

DAMPING = 0.05
EPSILON = 1e-06
MESH = pl.DeviceIdType.MESH
PARTS = 8
COLUMNS = 4
OWN, FIRST, SECOND, ACROSS = range(4)
NEAR = (2, -2, 1, -1)
LOTS = (slice(0, 1), slice(1, 3), slice(3, 4), slice(0, 2), slice(2, 4))
VMEM_BYTES = 40 * 1024 * 1024


def split(value):
    top = value.astype(jnp.bfloat16)
    return top, (value - top.astype(jnp.float32)).astype(jnp.bfloat16)


def product(left, right, contract):
    dims = (contract, ((), ()))
    total = None
    for i, a in enumerate(left):
        for b in right[: len(right) - i]:
            term = lax.dot_general(a, b, dims, preferred_element_type=jnp.float32)
            total = term if total is None else total + term
    return total


def precondition_slot(index, slot, q_ref, s_ref, a_ref, e_ref, rows_ref, turned_ref, blocks_ref):
    side = s_ref.shape[1]
    width = q_ref.shape[2]
    pieces = width // 128
    half = side // 2
    queries = q_ref[index].astype(jnp.float32)
    for piece in range(pieces):
        rows_ref[slot, 4 * piece : 4 * piece + 4, :] = queries[:, 128 * piece : 128 * (piece + 1)]
    basis = jnp.concatenate([s_ref[index, pl.ds(parity, half, stride=2), :] for parity in range(2)], axis=0)
    right = split(a_ref[index])
    scale = e_ref[index] + DAMPING
    stacked = []
    for n in range(4):
        both = rows_ref[slot, pl.ds(n, half, stride=4), :]
        stacked.append(jnp.concatenate([both[:, :side], both[:, side:]], axis=0))
    stacked = jnp.concatenate(stacked, axis=0)
    stacked = product((stacked.astype(jnp.bfloat16),), right, ((1,), (0,)))
    wide = jnp.concatenate([stacked[side * n : side * (n + 1)] for n in range(4)], axis=1)
    wide = product(split(basis.T), split(wide), ((1,), (0,)))
    wide = wide / jnp.concatenate([scale] * 4, axis=1)
    wide = product(split(basis), split(wide), ((1,), (0,)))
    stacked = jnp.concatenate([wide[:, side * n : side * (n + 1)] for n in range(4)], axis=0)
    stacked = product(split(stacked), right, ((1,), (1,)))
    for n in range(4):
        block = stacked[side * n : side * (n + 1)]
        turned_ref[slot, pl.ds(n, half, stride=4), :] = jnp.concatenate([block[:half], block[half:]], axis=1)
    for part in range(PARTS):
        blocks_ref[part, :, 128 * slot : 128 * (slot + 1)] = turned_ref[slot, 16 * part : 16 * (part + 1), :].astype(
            jnp.bfloat16
        )


def kernel(
    ring,
    groups,
    slot_hbm,
    q_hbm,
    s_hbm,
    a_hbm,
    e_hbm,
    train_ref,
    out_ref,
    slot_ref,
    q_ref,
    s_ref,
    a_ref,
    e_ref,
    rows_ref,
    turned_ref,
    blocks_ref,
    train_part,
    gathered,
    scored,
    tiles,
    tiles_in,
    summed,
    pair_out,
    pair_in,
    local_sem,
    t_send,
    t_recv,
    q_send,
    q_recv,
    near_send,
    near_recv,
    far_send,
    far_recv,
    across_send,
    across_recv,
    r_send,
    r_recv,
    p_send,
    p_recv,
):
    shard = lax.axis_index("shard")
    group = lax.axis_index("layer")
    core = lax.rem(group, 2)
    column = shard // ring
    level = lax.rem(shard, ring)
    slots = q_ref.shape[0]
    tile_count = tiles.shape[0]

    def at(col, lev):
        return col * ring + lev

    def shifted(by):
        return lax.rem(level + by + ring, ring)

    first = column + 1 - 2 * lax.rem(column, 2)
    second = 3 - column
    across = 3 - first
    columns = [column, first, second, across]

    def remote(src, dst, send, recv, to_shard, to_group=group):
        return pltpu.make_async_remote_copy(
            src_ref=src, dst_ref=dst, send_sem=send, recv_sem=recv, device_id=(to_shard, to_group), device_id_type=MESH
        )

    loads = []
    for i, (src, dst) in enumerate(
        [(q_hbm, q_ref), (a_hbm, a_ref), (s_hbm, s_ref), (e_hbm, e_ref), (slot_hbm, slot_ref)]
    ):
        copy = pltpu.make_async_copy(src, dst, local_sem.at[i])
        copy.start()
        loads.append(copy)


    barrier = pltpu.get_barrier_semaphore()
    partners = [(at(column, shifted(by)), group) for by in range(1, ring)]
    partners += [(at(c, level), group) for c in columns[1:]]
    for who in partners:
        pl.semaphore_signal(barrier, inc=1, device_id=who, device_id_type=MESH)

    def greet(d, carry):
        pl.semaphore_signal(barrier, inc=1, device_id=(shard, lax.rem(group + d, groups)), device_id_type=MESH)
        return carry

    lax.fori_loop(1, groups, greet, 0)
    span = train_ref.shape[2] // PARTS

    def part_of_train(part):
        return train_ref.at[:, :, pl.ds(pl.multiple_of(part * span, 128), span)]

    def train_to_column(who, half):
        i = 2 * who + half
        return remote(
            part_of_train(2 * columns[who] + half), train_part.at[i], t_send.at[i], t_recv.at[i], at(columns[who], level)
        )

    def train_to_level(i):
        to = shifted(-i)
        return remote(part_of_train(to), train_part.at[i], t_send.at[i], t_recv.at[i], at(column, to))

    def keep_for_column(half):
        return pltpu.make_async_copy(
            part_of_train(2 * column + half), train_part.at[half], local_sem.at[len(loads) + half]
        )

    def keep_for_level():
        return pltpu.make_async_copy(part_of_train(level), train_part.at[0], local_sem.at[len(loads)])

    @pl.when(core == 0)
    def _():
        for half in range(2):
            keep_for_column(half).start()

    @pl.when(core == 1)
    def _():
        keep_for_level().start()

    for copy in loads:
        copy.wait()
    for slot in range(slots):
        index = lax.rem(slot_ref[slot], slots)
        precondition_slot(index, slot, q_ref, s_ref, a_ref, e_ref, rows_ref, turned_ref, blocks_ref)

    pl.semaphore_wait(barrier, len(partners) + groups - 1)

    def score(whos, levels):
        many = whos.stop - whos.start
        count = many * len(levels)

        def blocks_of(part):
            value = [gathered[part, whos, pl.ds(lev, 1)].reshape(16 * many, 128 * slots) for lev in levels]
            return jnp.concatenate(value, axis=0) if len(value) > 1 else value[0]

        left = [blocks_of(part) for part in (0, 1 - core)]
        squares = [value.astype(jnp.float32) for value in left]
        squares = squares[0] * squares[0] + jnp.where(core == 0, squares[1] * squares[1], 0.0)
        norm = squares[:, :128]
        for slot in range(1, slots):
            norm = norm + squares[:, 128 * slot : 128 * (slot + 1)]
        lane = lax.broadcasted_iota(jnp.int32, (count, 8, 128), 2) // 32
        same = lax.broadcasted_iota(jnp.int32, (count, 16, 128), 1) // 4 == (
            lax.broadcasted_iota(jnp.int32, (count, 16, 128), 2) // 32
        )

        def queries_of(value):
            value = value[:, :8] + value[:, 8:]
            return value + pltpu.roll(value, 4, 1)

        low = jnp.zeros((count, 8, 128), jnp.float32)
        high = low
        for i in range(PARTS):
            right = jnp.concatenate(
                [
                    jnp.concatenate(
                        [train_part[i, slot, :, 128 * sub : 128 * (sub + 1)] for slot in range(slots)], axis=1
                    )
                    for sub in range(4)
                ],
                axis=0,
            )
            product = lax.dot_general(
                left[i % 2], right, (((1,), (1,)), ((), ())), preferred_element_type=jnp.float32
            ).reshape(count, 16, 128)
            value = queries_of(jnp.where(same, product, 0.0))
            value = value + pltpu.roll(value, 64, 2)
            value = value + pltpu.roll(value, 32, 2)
            low = low + jnp.where(lane == jnp.where(core == 0, i // 2, i), value, 0.0)
            if i >= 4:
                high = high + jnp.where(lane == i - 4, value, 0.0)
        norm = queries_of(norm.reshape(count, 16, 128))
        norm = jnp.broadcast_to(jnp.sum(norm, axis=2, keepdims=True), (count, 8, 128))
        for k, value in enumerate((low, high, norm)):
            for place, lev in enumerate(levels):
                scored[k, whos, pl.ds(lev, 1)] = value[many * place : many * (place + 1)].reshape(many, 1, 8, 128)

    def own_to_column(who):
        return remote(
            blocks_ref.at[pl.ds(2 * columns[who], 2)],
            gathered.at[:, who, level],
            q_send.at[who],
            q_recv.at[who],
            at(columns[who], level),
        )

    def block_of(lot, by):
        return gathered.at[:, LOTS[lot], shifted(by)]

    def near_copy(i, lot, source=0):
        block = block_of(lot, source)
        return remote(block, block, near_send.at[i, lot], near_recv.at[i, lot], at(column, shifted(NEAR[i])))

    def far_copy(row, lot, source, on):
        block = block_of(lot, source)
        return remote(block, block, far_send.at[row, lot], far_recv.at[row, lot], at(column, shifted(on)))

    far = [(row, lot, (-2, 2)[row], (1, -1)[row]) for lot in range(3) for row in range(2)]
    far += [(0, 3, -2, 2), (1, 4, 2, -2)]

    def own_to_level(i):
        to = shifted(-i)
        return remote(
            blocks_ref.at[to], gathered.at[0, OWN, level], q_send.at[i], q_recv.at[i], at(column, to)
        )

    def levels_to_column(who):
        return remote(
            gathered.at[0, OWN],
            gathered.at[0, who],
            across_send.at[who],
            across_recv.at[who],
            at(columns[who], level),
        )

    order = (4, 3, 5, 2, 6, 1, 7)

    @pl.when(core == 0)
    def _():
        for who in (FIRST, SECOND, ACROSS):
            own_to_column(who).start()
        for half in range(2):
            gathered[half, OWN, level] = blocks_ref[2 * column + half]
        for i in range(len(NEAR)):
            near_copy(i, 0).start()
        for half in range(2):
            for who in (ACROSS, FIRST, SECOND):
                train_to_column(who, half).start()
        for who in (FIRST, SECOND):
            own_to_column(who).wait_recv()
        for i in range(len(NEAR)):
            near_copy(i, 1).start()
        own_to_column(ACROSS).wait_recv()
        for i in range(len(NEAR)):
            near_copy(i, 2).start()
        for lot in range(3):
            for i in range(2):
                near_copy(i, lot, -NEAR[i]).wait_recv()
            for row, which, source, on in far:
                if which == lot or lot == 2 and which > 2:
                    far_copy(row, which, source, on).start()
        for lot in range(3):
            for i in range(2, len(NEAR)):
                near_copy(i, lot, -NEAR[i]).wait_recv()
        for half in range(2):
            keep_for_column(half).wait()
            for who in (FIRST, SECOND, ACROSS):
                train_to_column(who, half).wait_recv()
        score(slice(0, COLUMNS), [level] + [shifted(by) for by in NEAR])
        for row, lot, source, on in far:
            far_copy(row, lot, source - on, on).wait_recv()
        score(slice(0, COLUMNS), [shifted(by) for by in (3, 4, 5)])

    @pl.when(core == 1)
    def _():
        for i in order:
            own_to_level(i).start()
        for i in (1, 7, 2, 6, 3, 5, 4):
            train_to_level(i).start()
        gathered[0, OWN, level] = blocks_ref[level]
        for i in order:
            remote(
                blocks_ref.at[0],
                gathered.at[0, OWN, shifted(i)],
                q_send.at[i],
                q_recv.at[i],
                at(column, shifted(-i)),
            ).wait_recv()
        for who in (FIRST, SECOND, ACROSS):
            levels_to_column(who).start()
        keep_for_level().wait()
        for i in range(1, ring):
            train_to_level(i).wait_recv()
        score(slice(0, 1), list(range(ring)))
        for who in (ACROSS, FIRST, SECOND):
            levels_to_column(who).wait_recv()
        score(slice(1, COLUMNS), list(range(ring)))

    row = lax.broadcasted_iota(jnp.int32, (ring // 2, 8, 128), 1)
    per_column = tile_count // COLUMNS
    for who in range(COLUMNS):
        place = pl.ds(columns[who] * per_column, per_column)
        for k in range(3):
            value = scored[k, who].reshape(ring // 2, 2, 8, 128)
            tiles[place, :, 128 * k : 128 * (k + 1)] = jnp.where(row < 4, value[:, 0], value[:, 1])

    per_group = tile_count // groups

    def group_copy(d):
        to = lax.rem(group + d, groups)
        return remote(
            tiles.at[pl.ds(to * per_group, per_group)], tiles_in.at[d], r_send.at[d], r_recv.at[d], shard, to
        )

    for d in sorted(range(1, groups), key=lambda d: abs(2 * d - groups)):
        group_copy(d).start()

    def sum_of(which):
        def add(even):
            value = tiles[pl.ds(group * per_group, per_group)] if even else None
            for d in range(2 if even else 1, groups, 2):
                group_copy(d).wait_recv()
                value = tiles_in[d] if value is None else value + tiles_in[d]
            summed[which] = value

        @pl.when(core == which)
        def _():
            add(True)

        @pl.when(core != which)
        def _():
            add(False)

    is_score = lax.broadcasted_iota(jnp.int32, (per_group, 8, 128), 2) < 32

    def packed(j):
        which = 0 if j < COLUMNS else 1
        start = 128 if j >= COLUMNS + 4 else 0
        scores = summed[which, :, :, start : start + 128]
        turned = scores if j % 4 == 0 else pltpu.roll(scores, 128 - 32 * (j % 4), 2)
        return jnp.where(is_score, turned, summed[which, :, :, 256:])

    def pair_copy(j):
        to = at(columns[j], level) if j < COLUMNS else at(column, shifted(j - COLUMNS))
        return remote(pair_out.at[j], pair_in.at[j], p_send.at[j], p_recv.at[j], to)

    from_levels = [COLUMNS + i for i in (4, 3, 5, 2, 6, 1, 7)]
    from_columns = [ACROSS, FIRST, SECOND]
    others = from_levels + from_columns
    sum_of(1)
    for j in from_levels:
        pair_out[j] = packed(j)
        pair_copy(j).start()
    sum_of(0)
    for j in from_columns:
        pair_out[j] = packed(j)
        pair_copy(j).start()
    answer = packed(OWN) + packed(COLUMNS)
    for j in reversed(from_levels):
        pair_copy(j).wait_recv()
        answer = answer + pair_in[j]
    for j in reversed(from_columns):
        pair_copy(j).wait_recv()
        answer = answer + pair_in[j]
    out_ref[...] = (answer[:, :, :32] / jnp.sqrt(answer[:, :, 32:33] + EPSILON)).reshape(out_ref.shape)

    @pl.when(core == 0)
    def _():
        for half in range(2):
            for who in (FIRST, SECOND, ACROSS):
                train_to_column(who, half).wait_send()
        for who in (FIRST, SECOND, ACROSS):
            own_to_column(who).wait_send()
        for lot in range(3):
            for i in range(len(NEAR)):
                near_copy(i, lot).wait_send()
        for row, lot, source, on in far:
            far_copy(row, lot, source, on).wait_send()

    @pl.when(core == 1)
    def _():
        for i in range(1, ring):
            train_to_level(i).wait_send()
            own_to_level(i).wait_send()
        for who in (ACROSS, FIRST, SECOND):
            levels_to_column(who).wait_send()

    def tile_sent(d, carry):
        group_copy(d).wait_send()
        return carry

    lax.fori_loop(1, groups, tile_sent, 0)
    for j in others:
        pair_copy(j).wait_send()


def solution(mesh):
    shards, groups = mesh.shape["shard"], mesh.shape["layer"]
    ring = shards // COLUMNS

    def on_device(query_grads, out_basis, in_basis, eigen_scale, layer_slot, train_grads):
        local, slots, width = query_grads.shape
        side = out_basis.shape[1]
        rows = train_grads.shape[0]
        tile_count = local * shards // 8
        per_group = tile_count // groups
        dma = pltpu.SemaphoreType.DMA
        return pl.pallas_call(
            functools.partial(kernel, ring, groups),
            out_shape=jax.ShapeDtypeStruct((8 * per_group, rows), jnp.float32),
            in_specs=[pl.BlockSpec(memory_space=pl.ANY)] * 6,
            out_specs=pl.BlockSpec(memory_space=pltpu.VMEM),
            scratch_shapes=[
                pltpu.SMEM((slots,), jnp.int32),
                pltpu.VMEM((slots, local, width), jnp.bfloat16),
                pltpu.VMEM((slots, side, side), jnp.float32),
                pltpu.VMEM((slots, side, side), jnp.float32),
                pltpu.VMEM((slots, side, side), jnp.float32),
                pltpu.VMEM((slots, local * width // 128, 128), jnp.float32),
                pltpu.VMEM((slots, local * width // 128, 128), jnp.float32),
                pltpu.VMEM((PARTS, 16, 128 * slots), jnp.bfloat16),
                pltpu.VMEM((PARTS, slots, rows, width // PARTS), jnp.bfloat16),
                pltpu.VMEM((2, COLUMNS, ring, 16, 128 * slots), jnp.bfloat16),
                pltpu.VMEM((3, COLUMNS, ring, 8, 128), jnp.float32),
                pltpu.VMEM((tile_count, 8, 384), jnp.float32),
                pltpu.VMEM((groups, per_group, 8, 384), jnp.float32),
                pltpu.VMEM((2, per_group, 8, 384), jnp.float32),
                pltpu.VMEM((COLUMNS + ring, per_group, 8, 128), jnp.float32),
                pltpu.VMEM((COLUMNS + ring, per_group, 8, 128), jnp.float32),
                dma((7,)),
                dma((PARTS,)),
                dma((PARTS,)),
                dma((ring,)),
                dma((ring,)),
                dma((len(NEAR), 3)),
                dma((len(NEAR), 3)),
                dma((2, 5)),
                dma((2, 5)),
                dma((COLUMNS,)),
                dma((COLUMNS,)),
                dma((groups,)),
                dma((groups,)),
                dma((COLUMNS + ring,)),
                dma((COLUMNS + ring,)),
            ],
            compiler_params=pltpu.CompilerParams(
                collective_id=0, has_side_effects=True, vmem_limit_bytes=VMEM_BYTES
            ),
        )(
            *[
                pltpu.with_memory_space_constraint(x, pltpu.HBM)
                for x in (
                    layer_slot,
                    jnp.transpose(query_grads, (1, 0, 2)),
                    out_basis,
                    in_basis,
                    eigen_scale,
                    jnp.transpose(train_grads, (1, 0, 2)),
                )
            ]
        )

    return jax.shard_map(
        on_device,
        mesh=mesh,
        in_specs=(
            P("shard", "layer", None),
            P("layer", None, None),
            P("layer", None, None),
            P("layer", None, None),
            P("layer"),
            P("shard", "layer", None),
        ),
        out_specs=P("layer", "shard"),
        check_vma=False,
    )
```
